256 devices in a mesh: row: 16 (over x_lo, y, core), col: 16 (over x_hi, z).
Axes of the slice: x: 4 (x_hi: 2, x_lo: 2; x = x_hi * 2 + x_lo), y: 4, z: 8, core: 2. Of those that a mesh axis runs over, the one named last changes fastest.
Arguments:
- pair_act: bfloat16 [512, 512, 128], P('row', 'col'), may hold values from -6 to 6
- norm_gain: float32 [128], replicated, may hold values from 0.1 to 1.9
- norm_bias: float32 [128], replicated, may hold values from -3 to 3
- proj_weight: bfloat16 [128, 512], replicated, may hold values from -0.5 to 0.5
- proj_bias: float32 [512], replicated, may hold values from -3 to 3
- gate_weight: bfloat16 [128, 128], replicated, may hold values from -0.5 to 0.5
- gate_bias: float32 [128], replicated, may hold values from -3 to 3
- mid_gain: float32 [128], replicated, may hold values from 0.1 to 1.9
- mid_bias: float32 [128], replicated, may hold values from -3 to 3
- out_weight: bfloat16 [128, 128], replicated, may hold values from -0.5 to 0.5
- out_bias: float32 [128], replicated, may hold values from -3 to 3
Outputs:
- update: bfloat16 [512, 512, 128], P('row', 'col')
The draws below stay inside these ranges and needn't reach their ends.
All inputs are finite; a program needn't handle non-finite values.
Results may differ from the reference program's by a relative error of at most 0.0051.
Values may be sent and summed in bfloat16 or wider, within the bound.
A program may use at most 128 MiB of HBM per device.

```python
import jax
import jax.numpy as jnp
from jax import lax

C = 128
H = 128
N = 512


def level_of(rng, extent, pieces, low, high):
    loudness = 1.0
    for dim, shards_of in pieces:
        draws = jax.random.uniform(jax.random.fold_in(jax.random.fold_in(rng, 6), dim), (shards_of,), jnp.float32, low / len(pieces), high / len(pieces))
        loudness = loudness * jnp.repeat(jnp.exp(draws), extent[dim] // shards_of).reshape((-1,) + (1,) * (len(extent) - 1 - dim))
    return loudness


def normal_values(own_key, extent, width, limit, cuts=(), held_as=jnp.bfloat16):
    loudness = level_of(own_key, extent, cuts, -0.22, 0.18) if cuts else 1.0
    values = jax.random.normal(own_key, extent, jnp.float32) * width * loudness
    return jnp.minimum(jnp.maximum(values, -limit), limit).astype(held_as)


def setup_inputs(seed: int = 0) -> dict:
    splits = jax.random.split(jax.random.key(seed), 12)
    pair_act = normal_values(splits[0], (N, N, C), 1.0, 6.0, ((0, 16), (1, 16)))
    norm_gain = jnp.clip(1.0 + 0.18 * jax.random.normal(splits[1], (C,), jnp.float32), 0.1, 1.9)
    norm_bias = normal_values(splits[2], (C,), 0.5, 3.0, (), jnp.float32)
    proj_weight = normal_values(splits[3], (C, 4 * H), C ** -0.5, 0.5)
    proj_bias = normal_values(splits[4], (4 * H,), 0.5, 3.0, (), jnp.float32)
    gate_weight = normal_values(splits[5], (C, C), C ** -0.5, 0.5)
    gate_bias = normal_values(splits[6], (C,), 0.5, 3.0, (), jnp.float32)
    mid_gain = jnp.clip(1.0 + 0.18 * jax.random.normal(splits[7], (H,), jnp.float32), 0.1, 1.9)
    mid_bias = normal_values(splits[8], (H,), 0.5, 3.0, (), jnp.float32)
    out_weight = normal_values(splits[9], (H, C), H ** -0.5, 0.5)
    out_bias = normal_values(splits[10], (C,), 0.5, 3.0, (), jnp.float32)
    return dict(pair_act=pair_act, norm_gain=norm_gain, norm_bias=norm_bias, proj_weight=proj_weight, proj_bias=proj_bias, gate_weight=gate_weight, gate_bias=gate_bias, mid_gain=mid_gain, mid_bias=mid_bias, out_weight=out_weight, out_bias=out_bias)


def layer_norm(values, scale_vec, shift_vec):
    center = values - lax.optimization_barrier(jnp.mean(values, axis=-1, keepdims=True))
    spread = lax.optimization_barrier(jnp.mean(center * center, axis=-1, keepdims=True))
    return center * jax.lax.rsqrt(spread + 1e-05) * scale_vec + shift_vec

def reference(pair_act, norm_gain, norm_bias, proj_weight, proj_bias, gate_weight, gate_bias, mid_gain, mid_bias, out_weight, out_bias):
    normed = layer_norm(pair_act.astype(jnp.float32), norm_gain, norm_bias).astype(jnp.bfloat16)
    flat_norm = normed.reshape(N * N, C)
    projected = jnp.dot(flat_norm, proj_weight, preferred_element_type=jnp.float32) + proj_bias
    left_proj = (jax.nn.sigmoid(projected[:, :H]) * projected[:, H:2 * H]).astype(jnp.bfloat16).reshape(N, N, H)
    right_proj = (jax.nn.sigmoid(projected[:, 2 * H:3 * H]) * projected[:, 3 * H:]).astype(jnp.bfloat16).reshape(N, N, H)
    mixed_sum = jnp.einsum('kih,kjh->ijh', left_proj.astype(jnp.float32), right_proj.astype(jnp.float32))
    hidden_norm = layer_norm(mixed_sum, mid_gain, mid_bias).astype(jnp.bfloat16).reshape(N * N, H)
    gate_value = jax.nn.sigmoid(jnp.dot(flat_norm, gate_weight, preferred_element_type=jnp.float32) + gate_bias)
    outcome = jnp.dot(hidden_norm, out_weight, preferred_element_type=jnp.float32) + out_bias
    return (gate_value * outcome).astype(jnp.bfloat16).reshape(N, N, C)
```

```python
import jax
import jax.numpy as jnp
from jax import lax
from jax.experimental import pallas as pl
from jax.experimental.pallas import tpu as pltpu
from jax.sharding import PartitionSpec as P

MESH = pl.DeviceIdType.MESH
BF16 = jnp.bfloat16
F32 = jnp.float32
EPS = 1e-05

NX, NY, NZ = 4, 4, 8
CHIPS = NX * NY * NZ


def place():
    row, col = lax.axis_index("row"), lax.axis_index("col")
    core = lax.rem(row, 2)
    y = lax.rem(lax.div(row, 2), NY)
    x = lax.div(col, NZ) * 2 + lax.div(row, 2 * NY)
    return x, y, lax.rem(col, NZ), core


def device(x, y, z, core):
    return lax.rem(x, 2) * 8 + y * 2 + core, lax.div(x, 2) * NZ + z


def transpose_blocks(v, lane):
    low, even = lane < 64, lax.rem(lax.div(lane, 32), 2) == 0
    u0 = jnp.where(low, v[0], pltpu.roll(v[2], 64, 1))
    u2 = jnp.where(low, pltpu.roll(v[0], 64, 1), v[2])
    u1 = jnp.where(low, v[1], pltpu.roll(v[3], 64, 1))
    u3 = jnp.where(low, pltpu.roll(v[1], 64, 1), v[3])
    return (
        jnp.where(even, u0, pltpu.roll(u1, 32, 1)),
        jnp.where(even, pltpu.roll(u0, 96, 1), u1),
        jnp.where(even, u2, pltpu.roll(u3, 32, 1)),
        jnp.where(even, pltpu.roll(u2, 96, 1), u3),
    )


def column(vec, width):
    return jnp.transpose(jnp.broadcast_to(vec, (width, vec.shape[1])))


def kernel(
    x_ref, ng_ref, nb_ref, pw_ref, pb_ref, gw_ref, gb_ref, mg_ref, mb_ref, ow_ref, ob_ref,
    out_ref,
    xn, wt, pbt, grp, send, recv, left, right, part, part_in, total, back, back_in, mixed, gate,
    mgt, mbt, send_sem, recv_sem, part_send, part_recv, back_send, back_recv,
):
    x, y, z, core = place()
    rows, cols = device(x, y, z, core)
    slot = lax.div(rows, 2) * 16 + cols
    chan = (x * NY + y) * NZ + z
    partner = device(x, y, z, 1 - core)

    barrier = pltpu.get_barrier_semaphore()

    def greet(i, carry):
        dx, dy, dz = lax.div(i, 32), lax.rem(lax.div(i, 8), 4), lax.rem(i, 8)
        peer = device(lax.rem(x + dx, NX), lax.rem(y + dy, NY), lax.rem(z + dz, NZ), core)
        pl.semaphore_signal(barrier, inc=1, device_id=peer, device_id_type=MESH)
        return carry

    lax.fori_loop(1, CHIPS, greet, 0)
    pl.semaphore_signal(barrier, inc=1, device_id=partner, device_id_type=MESH)

    for t in range(8):
        chunk = pl.ds(t * 128, 128)
        v = x_ref[chunk, :].astype(F32)
        center = v - jnp.mean(v, axis=1, keepdims=True)
        spread = jnp.mean(center * center, axis=1, keepdims=True)
        xn[chunk, :] = (center * lax.rsqrt(spread + EPS) * ng_ref[...] + nb_ref[...]).astype(BF16)
    for t in range(4):
        wt[pl.ds(t * 128, 128), :] = jnp.transpose(pw_ref[:, t * 128 : (t + 1) * 128])
        pbt[pl.ds(t * 128, 128), :] = column(pb_ref[:, t * 128 : (t + 1) * 128], 128)

    pl.semaphore_wait(barrier, CHIPS)

    def project(i, carry):
        group = lax.rem(x * 2 + lax.div(y, 2) + 1 + i, 8)
        first = pl.multiple_of(group * 16, 16)
        weight = jnp.concatenate([wt[pl.ds(b * 128 + first, 16), :] for b in range(4)], axis=0)
        bias = [pbt[pl.ds(b * 128 + first, 16), :] for b in range(4)]
        for half in range(2):
            proj = lax.dot_general(
                weight,
                xn[pl.ds(half * 512, 512), :],
                (((1,), (1,)), ((), ())),
                preferred_element_type=F32,
            )
            for s in range(4):
                t = half * 4 + s
                p = [
                    proj[b * 16 : (b + 1) * 16, s * 128 : (s + 1) * 128] + bias[b]
                    for b in range(4)
                ]
                grp[pl.ds(t, 16, stride=16), :] = jax.nn.sigmoid(p[0]) * p[1]
                grp[pl.ds(8 + t, 16, stride=16), :] = jax.nn.sigmoid(p[2]) * p[3]
        send[pl.ds(first, 16)] = grp[...].reshape(16, 16, 128).astype(BF16)
        tx = lax.div(group, 2)
        for dy in range(2):
            ty = lax.rem(group, 2) * 2 + dy
            for dz in range(8):
                tz = lax.rem(z + dz, NZ)
                target = (tx * NY + ty) * NZ + tz

                def push(tx=tx, ty=ty, tz=tz, target=target):
                    pltpu.make_async_remote_copy(
                        src_ref=send.at[target],
                        dst_ref=recv.at[slot],
                        send_sem=send_sem,
                        recv_sem=recv_sem,
                        device_id=device(tx, ty, tz, core),
                        device_id_type=MESH,
                    ).start()

                if dz == 0:
                    pl.when(target != chan)(push)
                else:
                    push()
        return carry

    lax.fori_loop(0, 8, project, 0)
    recv[slot] = send[chan]

    for t in range(8):
        chunk = pl.ds(t * 128, 128)
        gate[chunk, :] = jax.nn.sigmoid(
            jnp.dot(xn[chunk, :], gw_ref[...], preferred_element_type=F32) + gb_ref[...]
        )
    mgt[...] = column(mg_ref[...], 128)
    mbt[...] = column(mb_ref[...], 128)

    sent = send.at[pl.ds(0, CHIPS - 1)]
    landed = recv.at[pl.ds(0, CHIPS - 1)]
    pltpu.make_async_copy(landed, landed, recv_sem).wait()

    lane = lax.broadcasted_iota(jnp.int32, (16, 128), 1)
    for p in range(4):
        for g in range(4):
            cs = [(g % 2) * 8 + 2 * m + g // 2 for m in range(4)]
            both = [
                [recv[(2 * p + q) * 16 + c].astype(F32) for q in range(2)] for c in cs
            ]
            for side, store in ((0, left), (8, right)):
                tiles = [
                    jnp.concatenate([one[side : side + 8] for one in pair], axis=0)
                    for pair in both
                ]
                for k4, tile in enumerate(transpose_blocks(tiles, lane)):
                    store[pl.ds(k4 * 64 + p * 16, 16), pl.ds(g * 128, 128)] = tile.astype(BF16)

    def product(which):
        start = pl.multiple_of(which * 256, 256)
        return lax.dot_general(
            left[:, pl.ds(start, 256)],
            right[...],
            (((0,), (0,)), ((), ())),
            preferred_element_type=F32,
        )

    part[...] = product(1 - core)
    swap = pltpu.make_async_remote_copy(
        src_ref=part,
        dst_ref=part_in,
        send_sem=part_send,
        recv_sem=part_recv,
        device_id=partner,
        device_id_type=MESH,
    )
    swap.start()
    total[...] = product(core)
    swap.wait_recv()

    lane8 = lax.broadcasted_iota(jnp.int32, (8, 128), 1)

    def give(i, carry):
        par = lax.rem(lax.rem(z, 2) + lax.div(i, 16), 2)
        tx = lax.rem(x + lax.div(lax.rem(i, 16), 4), NX)
        ty = lax.rem(y + lax.rem(i, 4), NY)
        b = lax.rem(tx, 2) * NY + ty
        g = par * 2 + lax.div(tx, 2)
        lanes = pl.ds(pl.multiple_of(g * 128, 128), 128)
        tiles = []
        for q in range(4):
            here = (pl.ds(pl.multiple_of(b * 32 + q * 8, 8), 8), lanes)
            tiles.append(total[here] + part_in[here])
        for m, tile in enumerate(transpose_blocks(tiles, lane8)):
            tz = 2 * m + par
            target = (tx * NY + ty) * NZ + tz
            back[target] = tile.astype(BF16)

            @pl.when(target != chan)
            def _(tz=tz, target=target):
                pltpu.make_async_remote_copy(
                    src_ref=back.at[target],
                    dst_ref=back_in.at[chan],
                    send_sem=back_send,
                    recv_sem=back_recv,
                    device_id=device(tx, ty, tz, core),
                    device_id_type=MESH,
                ).start()

        return carry

    lax.fori_loop(0, 32, give, 0)
    back_in[chan] = back[chan]

    gone = back.at[pl.ds(0, CHIPS - 1)]
    came = back_in.at[pl.ds(0, CHIPS - 1)]
    pltpu.make_async_copy(came, came, back_recv).wait()

    values = back_in[...].astype(F32)
    center = values - jnp.mean(values, axis=0, keepdims=True)
    spread = jnp.mean(center * center, axis=0, keepdims=True)
    mixed[...] = (center * lax.rsqrt(spread + EPS)).reshape(1024, 128)
    for t in range(8):
        norm = mixed[pl.ds(t, 128, stride=8), :] * mgt[...] + mbt[...]
        res = lax.dot_general(
            norm.astype(BF16),
            ow_ref[...],
            (((0,), (0,)), ((), ())),
            preferred_element_type=F32,
        ) + ob_ref[...]
        for q in range(4):
            where = pl.ds(q * 256 + t * 32, 32)
            out_ref[where, :] = (gate[where, :] * res[q * 32 : (q + 1) * 32]).astype(BF16)

    pltpu.make_async_copy(sent, sent, send_sem).wait()
    swap.wait_send()
    pltpu.make_async_copy(gone, gone, back_send).wait()


def per_device(
    pair_act, norm_gain, norm_bias, proj_weight, proj_bias, gate_weight, gate_bias, mid_gain,
    mid_bias, out_weight, out_bias,
):
    dma = pltpu.SemaphoreType.DMA
    vmem = pltpu.VMEM
    out = pl.pallas_call(
        kernel,
        out_shape=jax.ShapeDtypeStruct((1024, 128), BF16),
        in_specs=[pl.BlockSpec(memory_space=vmem)] * 11,
        out_specs=pl.BlockSpec(memory_space=vmem),
        scratch_shapes=[
            vmem((1024, 128), BF16),
            vmem((512, 128), BF16),
            vmem((512, 128), F32),
            vmem((256, 128), F32),
            vmem((CHIPS, 16, 128), BF16),
            vmem((CHIPS, 16, 128), BF16),
            vmem((256, 512), BF16),
            vmem((256, 512), BF16),
            vmem((256, 512), F32),
            vmem((256, 512), F32),
            vmem((256, 512), F32),
            vmem((CHIPS, 8, 128), BF16),
            vmem((CHIPS, 8, 128), BF16),
            vmem((1024, 128), F32),
            vmem((1024, 128), F32),
            vmem((128, 128), F32),
            vmem((128, 128), F32),
            dma, dma, dma, dma, dma, dma,
        ],
        compiler_params=pltpu.CompilerParams(
            collective_id=0, has_side_effects=True, vmem_limit_bytes=40 << 20
        ),
        cost_estimate=pl.CostEstimate(
            flops=500_000_000, bytes_accessed=2_000_000, transcendentals=1_000_000
        ),
        name="triangle",
    )(
        pair_act.reshape(1024, 128),
        norm_gain.reshape(1, -1),
        norm_bias.reshape(1, -1),
        proj_weight,
        proj_bias.reshape(1, -1),
        gate_weight,
        gate_bias.reshape(1, -1),
        mid_gain.reshape(1, -1),
        mid_bias.reshape(1, -1),
        out_weight,
        out_bias.reshape(1, -1),
    )
    return out.reshape(32, 32, 128)


def solution(mesh):
    placed = (P("row", "col", None),) + (P(),) * 10
    return jax.shard_map(
        per_device, mesh=mesh, in_specs=placed, out_specs=P("row", "col", None), check_vma=False
    )
```

```python
import jax
import jax.numpy as jnp
from jax import lax
from jax.experimental import pallas as pl
from jax.experimental.pallas import tpu as pltpu
from jax.sharding import PartitionSpec as P

MESH = pl.DeviceIdType.MESH
BF16 = jnp.bfloat16
F32 = jnp.float32
EPS = 1e-05

NX, NY, NZ = 4, 4, 8
CHIPS = NX * NY * NZ


def place():
    row, col = lax.axis_index("row"), lax.axis_index("col")
    core = lax.rem(row, 2)
    y = lax.rem(lax.div(row, 2), NY)
    x = lax.div(col, NZ) * 2 + lax.div(row, 2 * NY)
    return x, y, lax.rem(col, NZ), core


def device(x, y, z, core):
    return lax.rem(x, 2) * 8 + y * 2 + core, lax.div(x, 2) * NZ + z


def transpose_blocks(v, lane):
    low, even = lane < 64, lax.rem(lax.div(lane, 32), 2) == 0
    u0 = jnp.where(low, v[0], pltpu.roll(v[2], 64, 1))
    u2 = jnp.where(low, pltpu.roll(v[0], 64, 1), v[2])
    u1 = jnp.where(low, v[1], pltpu.roll(v[3], 64, 1))
    u3 = jnp.where(low, pltpu.roll(v[1], 64, 1), v[3])
    return (
        jnp.where(even, u0, pltpu.roll(u1, 32, 1)),
        jnp.where(even, pltpu.roll(u0, 96, 1), u1),
        jnp.where(even, u2, pltpu.roll(u3, 32, 1)),
        jnp.where(even, pltpu.roll(u2, 96, 1), u3),
    )


def column(vec, width):
    return jnp.transpose(jnp.broadcast_to(vec, (width, vec.shape[1])))


ORDER = (4, 3, 5, 2, 6, 1, 7, 0)
WAVES = ((3, 5), (4, 0), (2, 6), (1, 7))


def kernel(
    x_hbm, ng_hbm, nb_hbm, pw_hbm, pb_hbm, gw_hbm, gb_hbm, mg_hbm, mb_hbm, ow_hbm, ob_hbm,
    out_ref,
    x_ref, ng_ref, nb_ref, pw_ref, pb_ref, gw_ref, gb_ref, mg_ref, mb_ref, ow_ref, ob_ref, load_sem,
    xn, wt, pbt, grp_l, grp_r, send_l, send_r, recv_l, recv_r, left, left_t, right, part, part_in,
    total, back, back_in, mixed, gate, mgt, mbt,
    send_sem, left_sem, right_sem, part_send, part_recv, back_send, back_recv,
):
    loads = [
        pltpu.make_async_copy(src, dst, load_sem.at[i])
        for i, (src, dst) in enumerate(
            (
                (x_hbm, x_ref), (ng_hbm, ng_ref), (nb_hbm, nb_ref), (pw_hbm, pw_ref),
                (pb_hbm, pb_ref), (gw_hbm, gw_ref), (gb_hbm, gb_ref), (mg_hbm, mg_ref),
                (mb_hbm, mb_ref), (ow_hbm, ow_ref), (ob_hbm, ob_ref),
            )
        )
    ]
    for load in loads:
        load.start()
    x, y, z, core = place()
    rows, cols = device(x, y, z, core)
    slot = lax.div(rows, 2) * 16 + cols
    chan = z * 16 + x * NY + y
    partner = device(x, y, z, 1 - core)
    zs = [lax.rem(z + d, NZ) for d in range(NZ)]

    def each_plane(act):
        def step(i, carry):
            tx, ty = lax.rem(x + lax.div(i, 4) + 2, NX), lax.rem(y + lax.rem(i, 4) + 2, NY)
            act(i, tx, ty)
            return carry

        lax.fori_loop(0, 16, step, 0)

    barrier = pltpu.get_barrier_semaphore()

    def greet(i, tx, ty):
        for d in ORDER:

            def signal(tz=zs[d]):
                pl.semaphore_signal(
                    barrier, inc=1, device_id=device(tx, ty, tz, core), device_id_type=MESH
                )

            if d == 0:
                pl.when(i != 10)(signal)
            else:
                signal()

    each_plane(greet)
    pl.semaphore_signal(barrier, inc=1, device_id=partner, device_id_type=MESH)

    for load in loads:
        load.wait()
    for t in range(8):
        chunk = pl.ds(t * 128, 128)
        v = x_ref[chunk, :].astype(F32)
        center = v - jnp.mean(v, axis=1, keepdims=True)
        spread = jnp.mean(center * center, axis=1, keepdims=True)
        xn[chunk, :] = (center * lax.rsqrt(spread + EPS) * ng_ref[...] + nb_ref[...]).astype(BF16)
    for b in range(4):
        weight = jnp.transpose(pw_ref[:, b * 128 : (b + 1) * 128])
        bias = column(pb_ref[:, b * 128 : (b + 1) * 128], 128)
        for h in range(2):
            wt[pl.ds(h * 256 + b * 64, 64), :] = weight[h * 64 : (h + 1) * 64]
            pbt[pl.ds(h * 256 + b * 64, 64), :] = bias[h * 64 : (h + 1) * 64]

    def project(h):
        for pair in range(4):
            proj = lax.dot_general(
                wt[pl.ds(h * 256, 256), :],
                xn[pl.ds(pair * 256, 256), :],
                (((1,), (1,)), ((), ())),
                preferred_element_type=F32,
            )
            for s in range(2):
                t = pair * 2 + s
                p = [
                    proj[b * 64 : (b + 1) * 64, s * 128 : (s + 1) * 128]
                    + pbt[pl.ds(h * 256 + b * 64, 64), :]
                    for b in range(4)
                ]
                grp_l[pl.ds(t, 64, stride=8), :] = jax.nn.sigmoid(p[0]) * p[1]
                grp_r[pl.ds(t, 64, stride=8), :] = jax.nn.sigmoid(p[2]) * p[3]
        send_l[pl.ds(h * 64, 64)] = grp_l[...].reshape(64, 8, 128).astype(BF16)
        send_r[pl.ds(h * 64, 64)] = grp_r[...].reshape(64, 8, 128).astype(BF16)

    def spread_out(dzs, source, store, sem):
        def push(i, tx, ty):
            for d in dzs:
                target = zs[d] * 16 + tx * NY + ty

                def go(tz=zs[d], target=target):
                    pltpu.make_async_remote_copy(
                        src_ref=source.at[target],
                        dst_ref=store.at[slot],
                        send_sem=send_sem,
                        recv_sem=sem,
                        device_id=device(tx, ty, tz, core),
                        device_id_type=MESH,
                    ).start()

                if d == 0:
                    pl.when(i != 10)(go)
                else:
                    go()

        each_plane(push)

    project(0)
    project(1)

    pl.semaphore_wait(barrier, CHIPS)

    spread_out(ORDER, send_l, recv_l, left_sem)
    for w, wave in enumerate(WAVES):
        spread_out(wave, send_r, recv_r, right_sem.at[w])
    recv_l[slot] = send_l[chan]
    recv_r[slot] = send_r[chan]

    for t in range(8):
        chunk = pl.ds(t * 128, 128)
        gate[chunk, :] = jax.nn.sigmoid(
            jnp.dot(xn[chunk, :], gw_ref[...], preferred_element_type=F32) + gb_ref[...]
        )
    mgt[...] = column(mg_ref[...], 128)
    mbt[...] = column(mb_ref[...], 128)

    landed = recv_l.at[pl.ds(0, CHIPS - 1)]
    pltpu.make_async_copy(landed, landed, left_sem).wait()

    lane = lax.broadcasted_iota(jnp.int32, (16, 128), 1)

    def regroup(source, cs, store, first):
        for p in range(4):
            tiles = [
                jnp.concatenate(
                    [source[(2 * p + q) * 16 + c].astype(F32) for q in range(2)], axis=0
                )
                for c in cs
            ]
            for k4, tile in enumerate(transpose_blocks(tiles, lane)):
                store[pl.ds(k4 * 64 + p * 16, 16), pl.ds(first, 128)] = tile.astype(BF16)

    for g in range(4):
        regroup(recv_l, [(g % 2) * 8 + 2 * m + g // 2 for m in range(4)], left, g * 128)
    for g in range(4):
        for h in range(2):
            block = left[pl.ds(h * 128, 128), pl.ds(g * 128, 128)]
            left_t[pl.ds(g * 128, 128), pl.ds(h * 128, 128)] = jnp.transpose(block)

    lane8 = lax.broadcasted_iota(jnp.int32, (8, 128), 1)

    def product(which, w):
        start = pl.multiple_of(which * 256, 256)
        return jnp.dot(left_t[pl.ds(start, 256), :], right[w], preferred_element_type=F32)

    def multiply(w):
        wave = WAVES[w]
        arrived = recv_r.at[pl.ds(0, 31 if 0 in wave else 32)]
        pltpu.make_async_copy(arrived, arrived, right_sem.at[w]).wait()
        cs = [(m % 2) * 8 + zs[(8 - wave[m // 2]) % 8] for m in range(4)]
        regroup(recv_r, cs, right.at[w], 0)
        part[w] = product(1 - core, w)
        swap = pltpu.make_async_remote_copy(
            src_ref=part.at[w],
            dst_ref=part_in.at[w],
            send_sem=part_send.at[w],
            recv_sem=part_recv.at[w],
            device_id=partner,
            device_id_type=MESH,
        )
        swap.start()
        total[w] = product(core, w)
        return swap

    def give(w, swap):
        swap.wait_recv()
        places = []
        for i in range(8):
            lo, ty = lax.rem(x + 1 + i // 4, 2), lax.rem(y + 2 + i, NY)
            b = lo * NY + ty
            tiles = []
            for q in range(4):
                here = pl.ds(pl.multiple_of(b * 32 + q * 8, 8), 8)
                tiles.append(total[w, here, :] + part_in[w, here, :])
            for m, tile in enumerate(transpose_blocks(tiles, lane8)):
                tx, d = (m % 2) * 2 + lo, (8 - WAVES[w][m // 2]) % 8
                target = zs[d] * 16 + tx * NY + ty
                back[target] = tile.astype(BF16)
                places.append(((b * 2 + core, (m % 2) * NZ + zs[d]), target, d))
        for peer, target, d in places:

            def go(peer=peer, target=target):
                pltpu.make_async_remote_copy(
                    src_ref=back.at[target],
                    dst_ref=back_in.at[chan],
                    send_sem=back_send,
                    recv_sem=back_recv,
                    device_id=peer,
                    device_id_type=MESH,
                ).start()

            if d == 0:
                pl.when(target != chan)(go)
            else:
                go()

    swaps = [multiply(0), multiply(1)]
    give(0, swaps[0])
    swaps.append(multiply(2))
    give(1, swaps[1])
    swaps.append(multiply(3))
    give(2, swaps[2])
    give(3, swaps[3])
    back_in[chan] = back[chan]

    came = back_in.at[pl.ds(0, CHIPS - 1)]
    pltpu.make_async_copy(came, came, back_recv).wait()

    values = back_in[...].astype(F32)
    center = values - jnp.mean(values, axis=0, keepdims=True)
    spread = jnp.mean(center * center, axis=0, keepdims=True)
    mixed[...] = (center * lax.rsqrt(spread + EPS)).reshape(1024, 128)
    for t in range(8):
        norm = mixed[pl.ds(t, 128, stride=8), :] * mgt[...] + mbt[...]
        res = lax.dot_general(
            norm.astype(BF16),
            ow_ref[...],
            (((0,), (0,)), ((), ())),
            preferred_element_type=F32,
        ) + ob_ref[...]
        for q in range(4):
            where = pl.ds(q * 256 + t * 32, 32)
            out_ref[where, :] = (gate[where, :] * res[q * 32 : (q + 1) * 32]).astype(BF16)

    for sent in (send_l, send_r):
        gone = sent.at[pl.ds(0, CHIPS - 1)]
        pltpu.make_async_copy(gone, gone, send_sem).wait()
    for swap in swaps:
        swap.wait_send()
    gone = back.at[pl.ds(0, CHIPS - 1)]
    pltpu.make_async_copy(gone, gone, back_send).wait()


def per_device(
    pair_act, norm_gain, norm_bias, proj_weight, proj_bias, gate_weight, gate_bias, mid_gain,
    mid_bias, out_weight, out_bias,
):
    dma = pltpu.SemaphoreType.DMA
    vmem = pltpu.VMEM
    out = pl.pallas_call(
        kernel,
        out_shape=jax.ShapeDtypeStruct((1024, 128), BF16),
        in_specs=[pl.BlockSpec(memory_space=pl.ANY)] * 11,
        out_specs=pl.BlockSpec(memory_space=vmem),
        scratch_shapes=[
            vmem((1024, 128), BF16),
            vmem((1, 128), F32),
            vmem((1, 128), F32),
            vmem((128, 512), BF16),
            vmem((1, 512), F32),
            vmem((128, 128), BF16),
            vmem((1, 128), F32),
            vmem((1, 128), F32),
            vmem((1, 128), F32),
            vmem((128, 128), BF16),
            vmem((1, 128), F32),
            dma((11,)),
            vmem((1024, 128), BF16),
            vmem((512, 128), BF16),
            vmem((512, 128), F32),
            vmem((512, 128), F32),
            vmem((512, 128), F32),
            vmem((CHIPS, 8, 128), BF16),
            vmem((CHIPS, 8, 128), BF16),
            vmem((CHIPS, 8, 128), BF16),
            vmem((CHIPS, 8, 128), BF16),
            vmem((256, 512), BF16),
            vmem((512, 256), BF16),
            vmem((4, 256, 128), BF16),
            vmem((4, 256, 128), F32),
            vmem((4, 256, 128), F32),
            vmem((4, 256, 128), F32),
            vmem((CHIPS, 8, 128), BF16),
            vmem((CHIPS, 8, 128), BF16),
            vmem((1024, 128), F32),
            vmem((1024, 128), F32),
            vmem((128, 128), F32),
            vmem((128, 128), F32),
            dma, dma, dma((4,)), dma((4,)), dma((4,)), dma, dma,
        ],
        compiler_params=pltpu.CompilerParams(
            collective_id=0, has_side_effects=True, vmem_limit_bytes=56 << 20
        ),
        cost_estimate=pl.CostEstimate(
            flops=500_000_000, bytes_accessed=2_000_000, transcendentals=1_000_000
        ),
        name="triangle",
    )(
        pair_act.reshape(1024, 128),
        norm_gain.reshape(1, -1),
        norm_bias.reshape(1, -1),
        proj_weight,
        proj_bias.reshape(1, -1),
        gate_weight,
        gate_bias.reshape(1, -1),
        mid_gain.reshape(1, -1),
        mid_bias.reshape(1, -1),
        out_weight,
        out_bias.reshape(1, -1),
    )
    return out.reshape(32, 32, 128)


def solution(mesh):
    placed = (P("row", "col", None),) + (P(),) * 10
    return jax.shard_map(
        per_device, mesh=mesh, in_specs=placed, out_specs=P("row", "col", None), check_vma=False
    )
```

```python
import jax
import jax.numpy as jnp
from jax import lax
from jax.experimental import pallas as pl
from jax.experimental.pallas import tpu as pltpu
from jax.sharding import PartitionSpec as P

MESH = pl.DeviceIdType.MESH
BF16 = jnp.bfloat16
F32 = jnp.float32
EPS = 1e-05

NX, NY, NZ = 4, 4, 8
CHIPS = NX * NY * NZ


def place():
    row, col = lax.axis_index("row"), lax.axis_index("col")
    core = lax.rem(row, 2)
    y = lax.rem(lax.div(row, 2), NY)
    x = lax.div(col, NZ) * 2 + lax.div(row, 2 * NY)
    return x, y, lax.rem(col, NZ), core


def device(x, y, z, core):
    return lax.rem(x, 2) * 8 + y * 2 + core, lax.div(x, 2) * NZ + z


def transpose_blocks(v, lane):
    low, even = lane < 64, lax.rem(lax.div(lane, 32), 2) == 0
    u0 = jnp.where(low, v[0], pltpu.roll(v[2], 64, 1))
    u2 = jnp.where(low, pltpu.roll(v[0], 64, 1), v[2])
    u1 = jnp.where(low, v[1], pltpu.roll(v[3], 64, 1))
    u3 = jnp.where(low, pltpu.roll(v[1], 64, 1), v[3])
    return (
        jnp.where(even, u0, pltpu.roll(u1, 32, 1)),
        jnp.where(even, pltpu.roll(u0, 96, 1), u1),
        jnp.where(even, u2, pltpu.roll(u3, 32, 1)),
        jnp.where(even, pltpu.roll(u2, 96, 1), u3),
    )


def column(vec, width):
    return jnp.transpose(jnp.broadcast_to(vec, (width, vec.shape[1])))


WAVES = (
    ((1, 4), (1, 3), (1, 5), (0, 4)),
    ((1, 2), (1, 6), (0, 3), (0, 5)),
    ((1, 1), (1, 7), (0, 2), (0, 6)),
    ((1, 0), (0, 1), (0, 7), (0, 0)),
)
TO_CORE = (0, 1, 1, 0)
ROWS = (1, 0, 9, 8, 3, 2, 11, 10, 5, 4, 13, 12, 7, 6, 15, 14)


def kernel(
    x_hbm, ng_hbm, nb_hbm, pw_hbm, pb_hbm, gw_hbm, gb_hbm, mg_hbm, mb_hbm, ow_hbm, ob_hbm,
    out_hbm,
    x_ref, ng_ref, nb_ref, pw_ref, pb_ref, gw_ref, gb_ref, mg_ref, mb_ref, ow_ref, ob_ref, load_sem,
    xn, wt, pbt, grp_l, grp_r, send_l, send_r, recv_l, mate_l, recv_r, left, left_t, right, total,
    back, back_in, mixed, gate, mgt, mbt, result,
    send_sem, left_sem, right_sem, mate_send, mate_recv, back_send, back_recv, out_sem, mate_sem,
):
    loads = [
        pltpu.make_async_copy(src, dst, load_sem.at[i])
        for i, (src, dst) in enumerate(
            (
                (x_hbm, x_ref), (ng_hbm, ng_ref), (nb_hbm, nb_ref), (pw_hbm, pw_ref),
                (pb_hbm, pb_ref), (gw_hbm, gw_ref), (gb_hbm, gb_ref), (mg_hbm, mg_ref),
                (mb_hbm, mb_ref), (ow_hbm, ow_ref), (ob_hbm, ob_ref),
            )
        )
    ]
    for load in loads:
        load.start()
    x, y, z, core = place()
    rows, cols = device(x, y, z, core)
    slot = lax.div(rows, 2) * 16 + cols
    chan = z * 16 + x * NY + y
    partner = device(x, y, z, 1 - core)
    x_lo, x_hi = lax.rem(x, 2), lax.div(x, 2)

    def send_waves(act):
        for w, wave in enumerate(WAVES):
            chips = []
            for hi, d in wave:
                txh, tz = lax.rem(x_hi + hi, 2), lax.rem(z + d, NZ)
                chips.append(((hi, d) == (0, 0), tz * 16 + txh * 8, txh * NZ + tz))

            def step(i, carry, w=w, chips=chips):
                base = lax.rem(x_lo + 1 + lax.div(i, 4), 2) * NY + lax.rem(y + 2 + i, NY)
                for mine, to_chan, to_col in chips:
                    act(w, jnp.logical_and(i == 6, mine) if mine else None, base, to_chan, to_col)
                return carry

            lax.fori_loop(0, 8, step, 0)

    barrier = pltpu.get_barrier_semaphore()

    def greet(w, mine, base, to_chan, to_col):
        def signal():
            pl.semaphore_signal(
                barrier, inc=1, device_id=(base * 2 + core, to_col), device_id_type=MESH
            )

        if mine is None:
            signal()
        else:
            pl.when(jnp.logical_not(mine))(signal)

    send_waves(greet)
    pl.semaphore_signal(barrier, inc=1, device_id=partner, device_id_type=MESH)

    for load in loads:
        load.wait()
    for t in range(8):
        chunk = pl.ds(t * 128, 128)
        v = x_ref[chunk, :].astype(F32)
        center = v - jnp.mean(v, axis=1, keepdims=True)
        spread = jnp.mean(center * center, axis=1, keepdims=True)
        xn[chunk, :] = (center * lax.rsqrt(spread + EPS) * ng_ref[...] + nb_ref[...]).astype(BF16)
    for b in range(4):
        weight = jnp.transpose(pw_ref[:, b * 128 : (b + 1) * 128])
        bias = column(pb_ref[:, b * 128 : (b + 1) * 128], 128)
        for h in range(2):
            wt[pl.ds(h * 256 + b * 64, 64), :] = weight[h * 64 : (h + 1) * 64]
            pbt[pl.ds(h * 256 + b * 64, 64), :] = bias[h * 64 : (h + 1) * 64]

    def project(h):
        for pair in range(4):
            proj = lax.dot_general(
                wt[pl.ds(h * 256, 256), :],
                xn[pl.ds(pair * 256, 256), :],
                (((1,), (1,)), ((), ())),
                preferred_element_type=F32,
            )
            for s in range(2):
                t = pair * 2 + s
                p = [
                    proj[b * 64 : (b + 1) * 64, s * 128 : (s + 1) * 128]
                    + pbt[pl.ds(h * 256 + b * 64, 64), :]
                    for b in range(4)
                ]
                grp_l[pl.ds(t, 64, stride=8), :] = jax.nn.sigmoid(p[0]) * p[1]
                grp_r[pl.ds(t, 64, stride=8), :] = jax.nn.sigmoid(p[2]) * p[3]
        send_l[pl.ds(h * 64, 64)] = grp_l[...].reshape(64, 8, 128).astype(BF16)
        send_r[pl.ds(h * 64, 64)] = grp_r[...].reshape(64, 8, 128).astype(BF16)

    project(0)
    project(1)

    pl.semaphore_wait(barrier, CHIPS)
    pl.semaphore_signal(mate_sem, inc=1, device_id=partner, device_id_type=MESH)

    def push_left(w, mine, base, to_chan, to_col):
        def go():
            pltpu.make_async_remote_copy(
                src_ref=send_l.at[to_chan + base],
                dst_ref=recv_l.at[slot],
                send_sem=send_sem,
                recv_sem=left_sem,
                device_id=(base * 2 + core, to_col),
                device_id_type=MESH,
            ).start()

        if mine is None:
            go()
        else:
            pl.when(jnp.logical_not(mine))(go)

    def push_right(w, mine, base, to_chan, to_col):
        def go():
            pltpu.make_async_remote_copy(
                src_ref=send_r.at[to_chan + base],
                dst_ref=recv_r.at[core, slot],
                send_sem=send_sem,
                recv_sem=right_sem.at[w // 2],
                device_id=(base * 2 + TO_CORE[w], to_col),
                device_id_type=MESH,
            ).start()

        if mine is None:
            go()
        else:
            pl.when(jnp.logical_not(jnp.logical_and(mine, core == TO_CORE[w])))(go)

    send_waves(push_left)
    pl.semaphore_wait(mate_sem, 1)
    send_waves(push_right)
    recv_l[slot] = send_l[chan]

    @pl.when(core == TO_CORE[3])
    def _():
        pltpu.make_async_copy(send_r.at[chan], recv_r.at[core, slot], right_sem.at[1]).start()

    for t in range(8):
        chunk = pl.ds(t * 128, 128)
        gate[chunk, :] = jax.nn.sigmoid(
            jnp.dot(xn[chunk, :], gw_ref[...], preferred_element_type=F32) + gb_ref[...]
        )
    mgt[...] = column(mg_ref[...], 128)
    mbt[...] = column(mb_ref[...], 128)

    landed = recv_l.at[pl.ds(0, CHIPS - 1)]
    pltpu.make_async_copy(landed, landed, left_sem).wait()

    swap = pltpu.make_async_remote_copy(
        src_ref=recv_l,
        dst_ref=mate_l,
        send_sem=mate_send,
        recv_sem=mate_recv,
        device_id=partner,
        device_id_type=MESH,
    )
    swap.start()

    lane = lax.broadcasted_iota(jnp.int32, (16, 128), 1)

    def regroup(source, cs, store, row, first):
        for p in range(4):
            tiles = [
                jnp.concatenate(
                    [source[(2 * p + q) * 16 + c].astype(F32) for q in range(2)], axis=0
                )
                for c in cs
            ]
            for k4, tile in enumerate(transpose_blocks(tiles, lane)):
                store[pl.ds(row + k4 * 64 + p * 16, 16), pl.ds(first, 128)] = tile.astype(BF16)

    for half, source in enumerate((recv_l, mate_l)):
        if half == 1:
            swap.wait_recv()
        for g in range(4):
            regroup(source, [4 * g + m for m in range(4)], left, half * 256, g * 128)
        for g in range(4):
            for h in range(2):
                block = left[pl.ds(half * 256 + h * 128, 128), pl.ds(g * 128, 128)]
                left_t[pl.ds(g * 128, 128), pl.ds(half * 256 + h * 128, 128)] = jnp.transpose(block)

    lane8 = lax.broadcasted_iota(jnp.int32, (8, 128), 1)

    def multiply(j):
        arrived = recv_r.at[0, pl.ds(0, 64)]
        pltpu.make_async_copy(arrived, arrived, right_sem.at[j]).wait()
        for half, source in enumerate((recv_r.at[core], recv_r.at[1 - core])):
            regroup(source, came_from[j], right.at[j], half * 256, 0)
        total[j] = jnp.dot(left_t[...], right[j], preferred_element_type=F32)

    def give(j):
        places = []
        for i in range(16):
            row = ROWS[i]
            tiles = []
            for q in range(4):
                here = pl.ds(row * 32 + q * 8, 8)
                tiles.append(total[j, here, :])
            for m, tile in enumerate(transpose_blocks(tiles, lane8)):
                place_in = j * 64 + i * 4 + m
                back[place_in] = tile.astype(BF16)
                places.append((row, came_from[j][m], place_in, j == 1 and m == 3))
        for row, col, place_in, maybe_here in places:

            def go(row=row, col=col, place_in=place_in):
                pltpu.make_async_remote_copy(
                    src_ref=back.at[place_in],
                    dst_ref=back_in.at[chan],
                    send_sem=back_send,
                    recv_sem=back_recv,
                    device_id=(row, col),
                    device_id_type=MESH,
                ).start()

            if maybe_here:
                here = jnp.logical_and(row == rows, col == cols)
                pl.when(jnp.logical_not(here))(go)

                @pl.when(here)
                def _(place_in=place_in):
                    pltpu.make_async_copy(back.at[place_in], back_in.at[chan], back_recv).start()

            else:
                go()

    came_from = []
    for w0, w1 in ((0, 1), (3, 2)):
        cols_of = []
        for (hi0, d0), (hi1, d1) in zip(WAVES[w0], WAVES[w1]):
            hi, d = jnp.where(core == 0, hi0, hi1), jnp.where(core == 0, d0, d1)
            cols_of.append(lax.rem(x_hi + hi, 2) * NZ + lax.rem(z + NZ - d, NZ))
        came_from.append(cols_of)
    multiply(0)
    give(0)
    multiply(1)
    give(1)

    pltpu.make_async_copy(back_in, back_in, back_recv).wait()

    values = back_in[...].astype(F32)
    center = values - jnp.mean(values, axis=0, keepdims=True)
    spread = jnp.mean(center * center, axis=0, keepdims=True)
    mixed[...] = (center * lax.rsqrt(spread + EPS)).reshape(1024, 128)
    writes = []
    for t in range(8):
        norm = mixed[pl.ds(t, 128, stride=8), :] * mgt[...] + mbt[...]
        res = lax.dot_general(
            norm.astype(BF16),
            ow_ref[...],
            (((0,), (0,)), ((), ())),
            preferred_element_type=F32,
        ) + ob_ref[...]
        for q in range(4):
            where = pl.ds(q * 256 + t * 32, 32)
            result[q, t] = (gate[where, :] * res[q * 32 : (q + 1) * 32]).astype(BF16)
        if t % 2:
            pair = pl.ds(t - 1, 2)
            write = pltpu.make_async_copy(
                result.at[:, pair], out_hbm.at[:, pair], out_sem.at[t // 2]
            )
            write.start()
            writes.append(write)

    for write in writes:
        write.wait()
    swap.wait_send()
    for gone, sem in ((send_l, send_sem), (send_r, send_sem), (back, back_send)):
        most = gone.at[pl.ds(0, CHIPS - 1)]
        pltpu.make_async_copy(most, most, sem).wait()

    @pl.when(core != TO_CORE[3])
    def _():
        for gone, sem in ((send_r, send_sem), (back, back_send)):
            last = gone.at[pl.ds(0, 1)]
            pltpu.make_async_copy(last, last, sem).wait()


def per_device(
    pair_act, norm_gain, norm_bias, proj_weight, proj_bias, gate_weight, gate_bias, mid_gain,
    mid_bias, out_weight, out_bias,
):
    dma = pltpu.SemaphoreType.DMA
    vmem = pltpu.VMEM
    out = pl.pallas_call(
        kernel,
        out_shape=jax.ShapeDtypeStruct((4, 8, 32, 128), BF16),
        in_specs=[pl.BlockSpec(memory_space=pl.ANY)] * 11,
        out_specs=pl.BlockSpec(memory_space=pl.ANY),
        scratch_shapes=[
            vmem((1024, 128), BF16),
            vmem((1, 128), F32),
            vmem((1, 128), F32),
            vmem((128, 512), BF16),
            vmem((1, 512), F32),
            vmem((128, 128), BF16),
            vmem((1, 128), F32),
            vmem((1, 128), F32),
            vmem((1, 128), F32),
            vmem((128, 128), BF16),
            vmem((1, 128), F32),
            dma((11,)),
            vmem((1024, 128), BF16),
            vmem((512, 128), BF16),
            vmem((512, 128), F32),
            vmem((512, 128), F32),
            vmem((512, 128), F32),
            vmem((CHIPS, 8, 128), BF16),
            vmem((CHIPS, 8, 128), BF16),
            vmem((CHIPS, 8, 128), BF16),
            vmem((CHIPS, 8, 128), BF16),
            vmem((2, CHIPS, 8, 128), BF16),
            vmem((512, 512), BF16),
            vmem((512, 512), BF16),
            vmem((2, 512, 128), BF16),
            vmem((2, 512, 128), F32),
            vmem((CHIPS, 8, 128), BF16),
            vmem((CHIPS, 8, 128), BF16),
            vmem((1024, 128), F32),
            vmem((1024, 128), F32),
            vmem((128, 128), F32),
            vmem((128, 128), F32),
            vmem((4, 8, 32, 128), BF16),
            dma, dma, dma((2,)), dma, dma, dma, dma, dma((4,)), pltpu.SemaphoreType.REGULAR,
        ],
        compiler_params=pltpu.CompilerParams(
            collective_id=0, has_side_effects=True, vmem_limit_bytes=56 << 20
        ),
        cost_estimate=pl.CostEstimate(
            flops=500_000_000, bytes_accessed=2_000_000, transcendentals=1_000_000
        ),
        name="triangle",
    )(
        pair_act.reshape(1024, 128),
        norm_gain.reshape(1, -1),
        norm_bias.reshape(1, -1),
        proj_weight,
        proj_bias.reshape(1, -1),
        gate_weight,
        gate_bias.reshape(1, -1),
        mid_gain.reshape(1, -1),
        mid_bias.reshape(1, -1),
        out_weight,
        out_bias.reshape(1, -1),
    )
    return out.reshape(32, 32, 128)


def solution(mesh):
    placed = (P("row", "col", None),) + (P(),) * 10
    return jax.shard_map(
        per_device, mesh=mesh, in_specs=placed, out_specs=P("row", "col", None), check_vma=False
    )
```

```python
import jax
import jax.numpy as jnp
from jax import lax
from jax.experimental import pallas as pl
from jax.experimental.pallas import tpu as pltpu
from jax.sharding import PartitionSpec as P

MESH = pl.DeviceIdType.MESH
BF16 = jnp.bfloat16
F32 = jnp.float32
EPS = 1e-05

NX, NY, NZ = 4, 4, 8
CHIPS = NX * NY * NZ


def place():
    row, col = lax.axis_index("row"), lax.axis_index("col")
    core = lax.rem(row, 2)
    y = lax.rem(lax.div(row, 2), NY)
    x = lax.div(col, NZ) * 2 + lax.div(row, 2 * NY)
    return x, y, lax.rem(col, NZ), core


def device(x, y, z, core):
    return lax.rem(x, 2) * 8 + y * 2 + core, lax.div(x, 2) * NZ + z


def transpose_blocks(v, lane):
    low, even = lane < 64, lax.rem(lax.div(lane, 32), 2) == 0
    u0 = jnp.where(low, v[0], pltpu.roll(v[2], 64, 1))
    u2 = jnp.where(low, pltpu.roll(v[0], 64, 1), v[2])
    u1 = jnp.where(low, v[1], pltpu.roll(v[3], 64, 1))
    u3 = jnp.where(low, pltpu.roll(v[1], 64, 1), v[3])
    return (
        jnp.where(even, u0, pltpu.roll(u1, 32, 1)),
        jnp.where(even, pltpu.roll(u0, 96, 1), u1),
        jnp.where(even, u2, pltpu.roll(u3, 32, 1)),
        jnp.where(even, pltpu.roll(u2, 96, 1), u3),
    )


def column(vec, width):
    return jnp.transpose(jnp.broadcast_to(vec, (width, vec.shape[1])))


WAVES = (
    ((1, 4), (1, 3), (1, 5), (0, 4)),
    ((1, 2), (1, 6), (0, 3), (0, 5)),
    ((1, 1), (1, 7), (0, 2), (0, 6)),
    ((1, 0), (0, 1), (0, 7), (0, 0)),
)
TO_CORE = (0, 1, 1, 0)
ROWS = (1, 0, 9, 8, 3, 2, 11, 10, 5, 4, 13, 12, 7, 6, 15, 14)


def kernel(
    x_hbm, ng_hbm, nb_hbm, pw_hbm, pb_hbm, gw_hbm, gb_hbm,
    back_in, gate_hbm,
    x_ref, ng_ref, nb_ref, pw_ref, pb_ref, gw_ref, gb_ref, load_sem,
    xn, wt, pbt, grp_l, grp_r, send_l, send_r, recv_l, mate_l, recv_r, left, left_t, right, total,
    back, gate,
    send_sem, left_sem, right_sem, mate_send, mate_recv, back_send, back_recv, out_sem, mate_sem,
):
    loads = [
        pltpu.make_async_copy(src, dst, load_sem.at[i])
        for i, (src, dst) in enumerate(
            (
                (x_hbm, x_ref), (ng_hbm, ng_ref), (nb_hbm, nb_ref), (pw_hbm, pw_ref),
                (pb_hbm, pb_ref), (gw_hbm, gw_ref), (gb_hbm, gb_ref),
            )
        )
    ]
    for load in loads:
        load.start()
    x, y, z, core = place()
    rows, cols = device(x, y, z, core)
    slot = lax.div(rows, 2) * 16 + cols
    chan = z * 16 + x * NY + y
    partner = device(x, y, z, 1 - core)
    x_lo, x_hi = lax.rem(x, 2), lax.div(x, 2)

    def send_waves(act):
        for w, wave in enumerate(WAVES):
            chips = []
            for hi, d in wave:
                txh, tz = lax.rem(x_hi + hi, 2), lax.rem(z + d, NZ)
                chips.append(((hi, d) == (0, 0), tz * 16 + txh * 8, txh * NZ + tz))

            def step(i, carry, w=w, chips=chips):
                base = lax.rem(x_lo + 1 + lax.div(i, 4), 2) * NY + lax.rem(y + 2 + i, NY)
                for mine, to_chan, to_col in chips:
                    act(w, jnp.logical_and(i == 6, mine) if mine else None, base, to_chan, to_col)
                return carry

            lax.fori_loop(0, 8, step, 0)

    barrier = pltpu.get_barrier_semaphore()

    def greet(w, mine, base, to_chan, to_col):
        def signal():
            pl.semaphore_signal(
                barrier, inc=1, device_id=(base * 2 + core, to_col), device_id_type=MESH
            )

        if mine is None:
            signal()
        else:
            pl.when(jnp.logical_not(mine))(signal)

    send_waves(greet)
    pl.semaphore_signal(barrier, inc=1, device_id=partner, device_id_type=MESH)

    for load in loads:
        load.wait()
    for t in range(8):
        chunk = pl.ds(t * 128, 128)
        v = x_ref[chunk, :].astype(F32)
        center = v - jnp.mean(v, axis=1, keepdims=True)
        spread = jnp.mean(center * center, axis=1, keepdims=True)
        xn[chunk, :] = (center * lax.rsqrt(spread + EPS) * ng_ref[...] + nb_ref[...]).astype(BF16)
    for b in range(4):
        weight = jnp.transpose(pw_ref[:, b * 128 : (b + 1) * 128])
        bias = column(pb_ref[:, b * 128 : (b + 1) * 128], 128)
        for h in range(2):
            wt[pl.ds(h * 256 + b * 64, 64), :] = weight[h * 64 : (h + 1) * 64]
            pbt[pl.ds(h * 256 + b * 64, 64), :] = bias[h * 64 : (h + 1) * 64]

    def project(h):
        for pair in range(4):
            proj = lax.dot_general(
                wt[pl.ds(h * 256, 256), :],
                xn[pl.ds(pair * 256, 256), :],
                (((1,), (1,)), ((), ())),
                preferred_element_type=F32,
            )
            for s in range(2):
                t = pair * 2 + s
                p = [
                    proj[b * 64 : (b + 1) * 64, s * 128 : (s + 1) * 128]
                    + pbt[pl.ds(h * 256 + b * 64, 64), :]
                    for b in range(4)
                ]
                grp_l[pl.ds(t, 64, stride=8), :] = jax.nn.sigmoid(p[0]) * p[1]
                grp_r[pl.ds(t, 64, stride=8), :] = jax.nn.sigmoid(p[2]) * p[3]
        send_l[pl.ds(h * 64, 64)] = grp_l[...].reshape(64, 8, 128).astype(BF16)
        send_r[pl.ds(h * 64, 64)] = grp_r[...].reshape(64, 8, 128).astype(BF16)

    project(0)
    project(1)

    pl.semaphore_wait(barrier, CHIPS)
    pl.semaphore_signal(mate_sem, inc=1, device_id=partner, device_id_type=MESH)

    def push_left(w, mine, base, to_chan, to_col):
        def go():
            pltpu.make_async_remote_copy(
                src_ref=send_l.at[to_chan + base],
                dst_ref=recv_l.at[slot],
                send_sem=send_sem,
                recv_sem=left_sem,
                device_id=(base * 2 + core, to_col),
                device_id_type=MESH,
            ).start()

        if mine is None:
            go()
        else:
            pl.when(jnp.logical_not(mine))(go)

    def push_right(w, mine, base, to_chan, to_col):
        def go():
            pltpu.make_async_remote_copy(
                src_ref=send_r.at[to_chan + base],
                dst_ref=recv_r.at[core, slot],
                send_sem=send_sem,
                recv_sem=right_sem.at[w // 2],
                device_id=(base * 2 + TO_CORE[w], to_col),
                device_id_type=MESH,
            ).start()

        if mine is None:
            go()
        else:
            pl.when(jnp.logical_not(jnp.logical_and(mine, core == TO_CORE[w])))(go)

    send_waves(push_left)
    pl.semaphore_wait(mate_sem, 1)
    send_waves(push_right)
    recv_l[slot] = send_l[chan]

    @pl.when(core == TO_CORE[3])
    def _():
        pltpu.make_async_copy(send_r.at[chan], recv_r.at[core, slot], right_sem.at[1]).start()

    for t in range(8):
        chunk = pl.ds(t * 128, 128)
        gate[chunk, :] = jax.nn.sigmoid(
            jnp.dot(xn[chunk, :], gw_ref[...], preferred_element_type=F32) + gb_ref[...]
        )
    keep = pltpu.make_async_copy(gate, gate_hbm, out_sem)
    keep.start()

    landed = recv_l.at[pl.ds(0, CHIPS - 1)]
    pltpu.make_async_copy(landed, landed, left_sem).wait()

    swap = pltpu.make_async_remote_copy(
        src_ref=recv_l,
        dst_ref=mate_l,
        send_sem=mate_send,
        recv_sem=mate_recv,
        device_id=partner,
        device_id_type=MESH,
    )
    swap.start()

    lane = lax.broadcasted_iota(jnp.int32, (16, 128), 1)

    def regroup(source, cs, store, row, first):
        for p in range(4):
            tiles = [
                jnp.concatenate(
                    [source[(2 * p + q) * 16 + c].astype(F32) for q in range(2)], axis=0
                )
                for c in cs
            ]
            for k4, tile in enumerate(transpose_blocks(tiles, lane)):
                store[pl.ds(row + k4 * 64 + p * 16, 16), pl.ds(first, 128)] = tile.astype(BF16)

    for half, source in enumerate((recv_l, mate_l)):
        if half == 1:
            swap.wait_recv()
        for g in range(4):
            regroup(source, [4 * g + m for m in range(4)], left, half * 256, g * 128)
        for g in range(4):
            for h in range(2):
                block = left[pl.ds(half * 256 + h * 128, 128), pl.ds(g * 128, 128)]
                left_t[pl.ds(g * 128, 128), pl.ds(half * 256 + h * 128, 128)] = jnp.transpose(block)

    lane8 = lax.broadcasted_iota(jnp.int32, (8, 128), 1)

    def multiply(j):
        arrived = recv_r.at[0, pl.ds(0, 64)]
        pltpu.make_async_copy(arrived, arrived, right_sem.at[j]).wait()
        for half, source in enumerate((recv_r.at[core], recv_r.at[1 - core])):
            regroup(source, came_from[j], right.at[j], half * 256, 0)
        total[j] = jnp.dot(left_t[...], right[j], preferred_element_type=F32)

    def give(j):
        places = []
        for i in range(16):
            row = ROWS[i]
            tiles = []
            for q in range(4):
                here = pl.ds(row * 32 + q * 8, 8)
                tiles.append(total[j, here, :])
            for m, tile in enumerate(transpose_blocks(tiles, lane8)):
                place_in = j * 64 + i * 4 + m
                back[place_in] = tile.astype(BF16)
                places.append((row, came_from[j][m], place_in, j == 1 and m == 3))
        for row, col, place_in, maybe_here in places:

            def go(row=row, col=col, place_in=place_in):
                pltpu.make_async_remote_copy(
                    src_ref=back.at[place_in],
                    dst_ref=back_in.at[chan],
                    send_sem=back_send,
                    recv_sem=back_recv,
                    device_id=(row, col),
                    device_id_type=MESH,
                ).start()

            if maybe_here:
                here = jnp.logical_and(row == rows, col == cols)
                pl.when(jnp.logical_not(here))(go)

                @pl.when(here)
                def _(place_in=place_in):
                    pltpu.make_async_copy(back.at[place_in], back_in.at[chan], back_recv).start()

            else:
                go()

    came_from = []
    for w0, w1 in ((0, 1), (3, 2)):
        cols_of = []
        for (hi0, d0), (hi1, d1) in zip(WAVES[w0], WAVES[w1]):
            hi, d = jnp.where(core == 0, hi0, hi1), jnp.where(core == 0, d0, d1)
            cols_of.append(lax.rem(x_hi + hi, 2) * NZ + lax.rem(z + NZ - d, NZ))
        came_from.append(cols_of)
    multiply(0)
    give(0)
    multiply(1)
    give(1)

    pltpu.make_async_copy(back_in, back_in, back_recv).wait()

    keep.wait()
    swap.wait_send()
    for gone, sem in ((send_l, send_sem), (send_r, send_sem), (back, back_send)):
        most = gone.at[pl.ds(0, CHIPS - 1)]
        pltpu.make_async_copy(most, most, sem).wait()

    @pl.when(core != TO_CORE[3])
    def _():
        for gone, sem in ((send_r, send_sem), (back, back_send)):
            last = gone.at[pl.ds(0, 1)]
            pltpu.make_async_copy(last, last, sem).wait()


def finish(
    back_hbm, gate_hbm, mg_hbm, mb_hbm, ow_hbm, ob_hbm, out_hbm,
    back_in, gate, mg_ref, mb_ref, ow_ref, ob_ref, mixed, mgt, mbt, result, load_sem, out_sem,
):
    pieces = [
        pltpu.make_async_copy(
            back_hbm.at[pl.ds(i * 32, 32)], back_in.at[pl.ds(i * 32, 32)], load_sem.at[i]
        )
        for i in range(4)
    ]
    loads = [
        pltpu.make_async_copy(src, dst, load_sem.at[4 + i])
        for i, (src, dst) in enumerate(
            (
                (mg_hbm, mg_ref), (mb_hbm, mb_ref), (ow_hbm, ow_ref), (ob_hbm, ob_ref),
                (gate_hbm, gate),
            )
        )
    ]
    for load in pieces + loads:
        load.start()
    for load in loads[:2]:
        load.wait()
    mgt[...] = column(mg_ref[...], 128)
    mbt[...] = column(mb_ref[...], 128)
    for load in pieces:
        load.wait()
    values = back_in[...].astype(F32)
    center = values - jnp.mean(values, axis=0, keepdims=True)
    spread = jnp.mean(center * center, axis=0, keepdims=True)
    mixed[...] = (center * lax.rsqrt(spread + EPS)).reshape(1024, 128)
    for load in loads[2:]:
        load.wait()
    writes = []
    for t in range(8):
        norm = mixed[pl.ds(t, 128, stride=8), :] * mgt[...] + mbt[...]
        res = lax.dot_general(
            norm.astype(BF16),
            ow_ref[...],
            (((0,), (0,)), ((), ())),
            preferred_element_type=F32,
        ) + ob_ref[...]
        for q in range(4):
            where = pl.ds(q * 256 + t * 32, 32)
            result[q, t] = (gate[where, :] * res[q * 32 : (q + 1) * 32]).astype(BF16)
        if t % 2:
            pair = pl.ds(t - 1, 2)
            write = pltpu.make_async_copy(
                result.at[:, pair], out_hbm.at[:, pair], out_sem.at[t // 2]
            )
            write.start()
            writes.append(write)

    for write in writes:
        write.wait()


def per_device(
    pair_act, norm_gain, norm_bias, proj_weight, proj_bias, gate_weight, gate_bias, mid_gain,
    mid_bias, out_weight, out_bias,
):
    dma = pltpu.SemaphoreType.DMA
    vmem = pltpu.VMEM
    params = dict(has_side_effects=True, vmem_limit_bytes=56 << 20)
    blocks, gate = pl.pallas_call(
        kernel,
        out_shape=[
            jax.ShapeDtypeStruct((CHIPS, 8, 128), BF16),
            jax.ShapeDtypeStruct((1024, 128), F32),
        ],
        in_specs=[pl.BlockSpec(memory_space=pl.ANY)] * 7,
        out_specs=[pl.BlockSpec(memory_space=pl.ANY)] * 2,
        scratch_shapes=[
            vmem((1024, 128), BF16),
            vmem((1, 128), F32),
            vmem((1, 128), F32),
            vmem((128, 512), BF16),
            vmem((1, 512), F32),
            vmem((128, 128), BF16),
            vmem((1, 128), F32),
            dma((7,)),
            vmem((1024, 128), BF16),
            vmem((512, 128), BF16),
            vmem((512, 128), F32),
            vmem((512, 128), F32),
            vmem((512, 128), F32),
            vmem((CHIPS, 8, 128), BF16),
            vmem((CHIPS, 8, 128), BF16),
            vmem((CHIPS, 8, 128), BF16),
            vmem((CHIPS, 8, 128), BF16),
            vmem((2, CHIPS, 8, 128), BF16),
            vmem((512, 512), BF16),
            vmem((512, 512), BF16),
            vmem((2, 512, 128), BF16),
            vmem((2, 512, 128), F32),
            vmem((CHIPS, 8, 128), BF16),
            vmem((1024, 128), F32),
            dma, dma, dma((2,)), dma, dma, dma, dma, dma, pltpu.SemaphoreType.REGULAR,
        ],
        compiler_params=pltpu.CompilerParams(collective_id=0, **params),
        cost_estimate=pl.CostEstimate(
            flops=500_000_000, bytes_accessed=2_000_000, transcendentals=1_000_000
        ),
        name="triangle",
    )(
        pair_act.reshape(1024, 128),
        norm_gain.reshape(1, -1),
        norm_bias.reshape(1, -1),
        proj_weight,
        proj_bias.reshape(1, -1),
        gate_weight,
        gate_bias.reshape(1, -1),
    )
    out = pl.pallas_call(
        finish,
        out_shape=jax.ShapeDtypeStruct((4, 8, 32, 128), BF16),
        in_specs=[pl.BlockSpec(memory_space=pl.ANY)] * 6,
        out_specs=pl.BlockSpec(memory_space=pl.ANY),
        scratch_shapes=[
            vmem((CHIPS, 8, 128), BF16),
            vmem((1024, 128), F32),
            vmem((1, 128), F32),
            vmem((1, 128), F32),
            vmem((128, 128), BF16),
            vmem((1, 128), F32),
            vmem((1024, 128), F32),
            vmem((128, 128), F32),
            vmem((128, 128), F32),
            vmem((4, 8, 32, 128), BF16),
            dma((9,)),
            dma((4,)),
        ],
        compiler_params=pltpu.CompilerParams(vmem_limit_bytes=56 << 20),
        name="finish",
    )(blocks, gate, mid_gain.reshape(1, -1), mid_bias.reshape(1, -1), out_weight, out_bias.reshape(1, -1))
    return out.reshape(32, 32, 128)


def solution(mesh):
    placed = (P("row", "col", None),) + (P(),) * 10
    return jax.shard_map(
        per_device, mesh=mesh, in_specs=placed, out_specs=P("row", "col", None), check_vma=False
    )
```

```python
import jax
import jax.numpy as jnp
from jax import lax
from jax.experimental import pallas as pl
from jax.experimental.pallas import tpu as pltpu
from jax.sharding import PartitionSpec as P

MESH = pl.DeviceIdType.MESH
BF16 = jnp.bfloat16
F32 = jnp.float32
EPS = 1e-05

NX, NY, NZ = 4, 4, 8
CHIPS = NX * NY * NZ


def place():
    row, col = lax.axis_index("row"), lax.axis_index("col")
    core = lax.rem(row, 2)
    y = lax.rem(lax.div(row, 2), NY)
    x = lax.div(col, NZ) * 2 + lax.div(row, 2 * NY)
    return x, y, lax.rem(col, NZ), core


def device(x, y, z, core):
    return lax.rem(x, 2) * 8 + y * 2 + core, lax.div(x, 2) * NZ + z


def transpose_blocks(v, lane):
    low, even = lane < 64, lax.rem(lax.div(lane, 32), 2) == 0
    u0 = jnp.where(low, v[0], pltpu.roll(v[2], 64, 1))
    u2 = jnp.where(low, pltpu.roll(v[0], 64, 1), v[2])
    u1 = jnp.where(low, v[1], pltpu.roll(v[3], 64, 1))
    u3 = jnp.where(low, pltpu.roll(v[1], 64, 1), v[3])
    return (
        jnp.where(even, u0, pltpu.roll(u1, 32, 1)),
        jnp.where(even, pltpu.roll(u0, 96, 1), u1),
        jnp.where(even, u2, pltpu.roll(u3, 32, 1)),
        jnp.where(even, pltpu.roll(u2, 96, 1), u3),
    )


def column(vec, width):
    return jnp.transpose(jnp.broadcast_to(vec, (width, vec.shape[1])))


WAVES = (
    ((1, 4), (1, 3), (1, 5), (0, 4)),
    ((1, 2), (1, 6), (0, 3), (0, 5)),
    ((1, 1), (1, 7), (0, 2), (0, 6)),
    ((1, 0), (0, 1), (0, 7), (0, 0)),
)
TO_CORE = (0, 1, 1, 0)
ROWS = (1, 0, 9, 8, 3, 2, 11, 10, 5, 4, 13, 12, 7, 6, 15, 14)


def kernel(
    x_hbm, ng_hbm, nb_hbm, pw_hbm, pb_hbm, gw_hbm, gb_hbm,
    back_in, gate_hbm,
    x_ref, ng_ref, nb_ref, pw_ref, pb_ref, gw_ref, gb_ref, load_sem,
    xn, wt, pbt, grp_l, grp_r, send_l, send_r, recv_l, mate_l, recv_r, left, left_t, right, total,
    back, gate,
    send_sem, left_sem, right_sem, mate_send, mate_recv, back_send, back_recv, out_sem, mate_sem,
):
    loads = [
        pltpu.make_async_copy(src, dst, load_sem.at[i])
        for i, (src, dst) in enumerate(
            (
                (x_hbm, x_ref), (ng_hbm, ng_ref), (nb_hbm, nb_ref), (pw_hbm, pw_ref),
                (pb_hbm, pb_ref), (gw_hbm, gw_ref), (gb_hbm, gb_ref),
            )
        )
    ]
    for load in loads:
        load.start()
    x, y, z, core = place()
    rows, cols = device(x, y, z, core)
    slot = lax.div(rows, 2) * 16 + cols
    chan = z * 16 + x * NY + y
    partner = device(x, y, z, 1 - core)
    x_lo, x_hi = lax.rem(x, 2), lax.div(x, 2)

    def send_waves(act, waves=(0, 1, 2, 3)):
        for w in waves:
            wave = WAVES[w]
            chips = []
            for hi, d in wave:
                txh, tz = lax.rem(x_hi + hi, 2), lax.rem(z + d, NZ)
                chips.append(((hi, d) == (0, 0), tz * 16 + txh * 8, txh * NZ + tz))

            def step(i, carry, w=w, chips=chips):
                base = lax.rem(x_lo + 1 + lax.div(i, 4), 2) * NY + lax.rem(y + 2 + i, NY)
                for mine, to_chan, to_col in chips:
                    act(w, jnp.logical_and(i == 6, mine) if mine else None, base, to_chan, to_col)
                return carry

            lax.fori_loop(0, 8, step, 0)

    barrier = pltpu.get_barrier_semaphore()

    def greet(w, mine, base, to_chan, to_col):
        def signal():
            pl.semaphore_signal(
                barrier, inc=1, device_id=(base * 2 + core, to_col), device_id_type=MESH
            )

        if mine is None:
            signal()
        else:
            pl.when(jnp.logical_not(mine))(signal)

    send_waves(greet)
    pl.semaphore_signal(barrier, inc=1, device_id=partner, device_id_type=MESH)

    for load in loads:
        load.wait()
    for t in range(8):
        chunk = pl.ds(t * 128, 128)
        v = x_ref[chunk, :].astype(F32)
        center = v - jnp.mean(v, axis=1, keepdims=True)
        spread = jnp.mean(center * center, axis=1, keepdims=True)
        xn[chunk, :] = (center * lax.rsqrt(spread + EPS) * ng_ref[...] + nb_ref[...]).astype(BF16)
    for b in range(4):
        weight = jnp.transpose(pw_ref[:, b * 128 : (b + 1) * 128])
        bias = column(pb_ref[:, b * 128 : (b + 1) * 128], 128)
        for h in range(2):
            wt[pl.ds(h * 256 + b * 64, 64), :] = weight[h * 64 : (h + 1) * 64]
            pbt[pl.ds(h * 256 + b * 64, 64), :] = bias[h * 64 : (h + 1) * 64]

    def project(h):
        for pair in range(4):
            proj = lax.dot_general(
                wt[pl.ds(h * 256, 256), :],
                xn[pl.ds(pair * 256, 256), :],
                (((1,), (1,)), ((), ())),
                preferred_element_type=F32,
            )
            for s in range(2):
                t = pair * 2 + s
                p = [
                    proj[b * 64 : (b + 1) * 64, s * 128 : (s + 1) * 128]
                    + pbt[pl.ds(h * 256 + b * 64, 64), :]
                    for b in range(4)
                ]
                grp_l[pl.ds(t, 64, stride=8), :] = jax.nn.sigmoid(p[0]) * p[1]
                grp_r[pl.ds(t, 64, stride=8), :] = jax.nn.sigmoid(p[2]) * p[3]
        send_l[pl.ds(h * 64, 64)] = grp_l[...].reshape(64, 8, 128).astype(BF16)
        send_r[pl.ds(h * 64, 64)] = grp_r[...].reshape(64, 8, 128).astype(BF16)

    project(0)
    project(1)

    pl.semaphore_wait(barrier, CHIPS)
    pl.semaphore_signal(mate_sem, inc=1, device_id=partner, device_id_type=MESH)

    def push_left(w, mine, base, to_chan, to_col):
        def go():
            pltpu.make_async_remote_copy(
                src_ref=send_l.at[to_chan + base],
                dst_ref=recv_l.at[slot],
                send_sem=send_sem,
                recv_sem=left_sem,
                device_id=(base * 2 + core, to_col),
                device_id_type=MESH,
            ).start()

        if mine is None:
            go()
        else:
            pl.when(jnp.logical_not(mine))(go)

    def push_right(w, mine, base, to_chan, to_col):
        def go():
            pltpu.make_async_remote_copy(
                src_ref=send_r.at[to_chan + base],
                dst_ref=recv_r.at[core, slot],
                send_sem=send_sem,
                recv_sem=right_sem.at[w // 2],
                device_id=(base * 2 + TO_CORE[w], to_col),
                device_id_type=MESH,
            ).start()

        if mine is None:
            go()
        else:
            pl.when(jnp.logical_not(jnp.logical_and(mine, core == TO_CORE[w])))(go)

    send_waves(push_left, (0, 1, 3, 2))
    pl.semaphore_wait(mate_sem, 1)
    send_waves(push_right, (2, 3, 0, 1))
    recv_l[slot] = send_l[chan]

    @pl.when(core == TO_CORE[3])
    def _():
        pltpu.make_async_copy(send_r.at[chan], recv_r.at[core, slot], right_sem.at[1]).start()

    for t in range(8):
        chunk = pl.ds(t * 128, 128)
        gate[chunk, :] = jax.nn.sigmoid(
            jnp.dot(xn[chunk, :], gw_ref[...], preferred_element_type=F32) + gb_ref[...]
        )
    keep = pltpu.make_async_copy(gate, gate_hbm, out_sem)
    keep.start()

    landed = recv_l.at[pl.ds(0, CHIPS - 1)]
    pltpu.make_async_copy(landed, landed, left_sem).wait()

    swap = pltpu.make_async_remote_copy(
        src_ref=recv_l,
        dst_ref=mate_l,
        send_sem=mate_send,
        recv_sem=mate_recv,
        device_id=partner,
        device_id_type=MESH,
    )
    swap.start()

    lane = lax.broadcasted_iota(jnp.int32, (16, 128), 1)

    def regroup(source, cs, store, row, first):
        for p in range(4):
            tiles = [
                jnp.concatenate(
                    [source[(2 * p + q) * 16 + c].astype(F32) for q in range(2)], axis=0
                )
                for c in cs
            ]
            for k4, tile in enumerate(transpose_blocks(tiles, lane)):
                store[pl.ds(row + k4 * 64 + p * 16, 16), pl.ds(first, 128)] = tile.astype(BF16)

    for half, source in enumerate((recv_l, mate_l)):
        if half == 1:
            swap.wait_recv()
        for g in range(4):
            regroup(source, [4 * g + m for m in range(4)], left, half * 256, g * 128)
        for g in range(4):
            for h in range(2):
                block = left[pl.ds(half * 256 + h * 128, 128), pl.ds(g * 128, 128)]
                left_t[pl.ds(g * 128, 128), pl.ds(half * 256 + h * 128, 128)] = jnp.transpose(block)

    lane8 = lax.broadcasted_iota(jnp.int32, (8, 128), 1)

    def multiply(j):
        arrived = recv_r.at[0, pl.ds(0, 64)]
        pltpu.make_async_copy(arrived, arrived, right_sem.at[j]).wait()
        for half, source in enumerate((recv_r.at[core], recv_r.at[1 - core])):
            regroup(source, came_from[j], right.at[j], half * 256, 0)
        total[j] = jnp.dot(left_t[...], right[j], preferred_element_type=F32)

    def give(j):
        places = []
        for i in range(16):
            row = ROWS[i]
            tiles = []
            for q in range(4):
                here = pl.ds(row * 32 + q * 8, 8)
                tiles.append(total[j, here, :])
            for m, tile in enumerate(transpose_blocks(tiles, lane8)):
                place_in = j * 64 + i * 4 + m
                back[place_in] = tile.astype(BF16)
                places.append((row, came_from[j][m], place_in, j == 1 and m == 3))
        for row, col, place_in, maybe_here in places:

            def go(row=row, col=col, place_in=place_in):
                pltpu.make_async_remote_copy(
                    src_ref=back.at[place_in],
                    dst_ref=back_in.at[chan],
                    send_sem=back_send,
                    recv_sem=back_recv,
                    device_id=(row, col),
                    device_id_type=MESH,
                ).start()

            if maybe_here:
                here = jnp.logical_and(row == rows, col == cols)
                pl.when(jnp.logical_not(here))(go)

                @pl.when(here)
                def _(place_in=place_in):
                    pltpu.make_async_copy(back.at[place_in], back_in.at[chan], back_recv).start()

            else:
                go()

    came_from = []
    for w0, w1 in ((0, 1), (3, 2)):
        cols_of = []
        for (hi0, d0), (hi1, d1) in zip(WAVES[w0], WAVES[w1]):
            hi, d = jnp.where(core == 0, hi0, hi1), jnp.where(core == 0, d0, d1)
            cols_of.append(lax.rem(x_hi + hi, 2) * NZ + lax.rem(z + NZ - d, NZ))
        came_from.append(cols_of)
    multiply(1)
    give(1)
    multiply(0)
    give(0)

    pltpu.make_async_copy(back_in, back_in, back_recv).wait()

    keep.wait()
    swap.wait_send()
    for gone, sem in ((send_l, send_sem), (send_r, send_sem), (back, back_send)):
        most = gone.at[pl.ds(0, CHIPS - 1)]
        pltpu.make_async_copy(most, most, sem).wait()

    @pl.when(core != TO_CORE[3])
    def _():
        for gone, sem in ((send_r, send_sem), (back, back_send)):
            last = gone.at[pl.ds(0, 1)]
            pltpu.make_async_copy(last, last, sem).wait()


def finish(
    back_hbm, gate_hbm, mg_hbm, mb_hbm, ow_hbm, ob_hbm, out_hbm,
    back_in, gate, mg_ref, mb_ref, ow_ref, ob_ref, mixed, mgt, mbt, result, load_sem, out_sem,
):
    pieces = [
        pltpu.make_async_copy(
            back_hbm.at[pl.ds(i * 32, 32)], back_in.at[pl.ds(i * 32, 32)], load_sem.at[i]
        )
        for i in range(4)
    ]
    loads = [
        pltpu.make_async_copy(src, dst, load_sem.at[4 + i])
        for i, (src, dst) in enumerate(
            (
                (mg_hbm, mg_ref), (mb_hbm, mb_ref), (ow_hbm, ow_ref), (ob_hbm, ob_ref),
                (gate_hbm, gate),
            )
        )
    ]
    for load in pieces + loads:
        load.start()
    for load in loads[:2]:
        load.wait()
    mgt[...] = column(mg_ref[...], 128)
    mbt[...] = column(mb_ref[...], 128)
    for load in pieces:
        load.wait()
    values = back_in[...].astype(F32)
    center = values - jnp.mean(values, axis=0, keepdims=True)
    spread = jnp.mean(center * center, axis=0, keepdims=True)
    mixed[...] = (center * lax.rsqrt(spread + EPS)).reshape(1024, 128)
    for load in loads[2:]:
        load.wait()
    writes = []
    for t in range(8):
        norm = mixed[pl.ds(t, 128, stride=8), :] * mgt[...] + mbt[...]
        res = lax.dot_general(
            norm.astype(BF16),
            ow_ref[...],
            (((0,), (0,)), ((), ())),
            preferred_element_type=F32,
        ) + ob_ref[...]
        for q in range(4):
            where = pl.ds(q * 256 + t * 32, 32)
            result[q, t] = (gate[where, :] * res[q * 32 : (q + 1) * 32]).astype(BF16)
        if t % 2:
            pair = pl.ds(t - 1, 2)
            write = pltpu.make_async_copy(
                result.at[:, pair], out_hbm.at[:, pair], out_sem.at[t // 2]
            )
            write.start()
            writes.append(write)

    for write in writes:
        write.wait()


def per_device(
    pair_act, norm_gain, norm_bias, proj_weight, proj_bias, gate_weight, gate_bias, mid_gain,
    mid_bias, out_weight, out_bias,
):
    dma = pltpu.SemaphoreType.DMA
    vmem = pltpu.VMEM
    params = dict(has_side_effects=True, vmem_limit_bytes=56 << 20)
    blocks, gate = pl.pallas_call(
        kernel,
        out_shape=[
            jax.ShapeDtypeStruct((CHIPS, 8, 128), BF16),
            jax.ShapeDtypeStruct((1024, 128), F32),
        ],
        in_specs=[pl.BlockSpec(memory_space=pl.ANY)] * 7,
        out_specs=[pl.BlockSpec(memory_space=pl.ANY)] * 2,
        scratch_shapes=[
            vmem((1024, 128), BF16),
            vmem((1, 128), F32),
            vmem((1, 128), F32),
            vmem((128, 512), BF16),
            vmem((1, 512), F32),
            vmem((128, 128), BF16),
            vmem((1, 128), F32),
            dma((7,)),
            vmem((1024, 128), BF16),
            vmem((512, 128), BF16),
            vmem((512, 128), F32),
            vmem((512, 128), F32),
            vmem((512, 128), F32),
            vmem((CHIPS, 8, 128), BF16),
            vmem((CHIPS, 8, 128), BF16),
            vmem((CHIPS, 8, 128), BF16),
            vmem((CHIPS, 8, 128), BF16),
            vmem((2, CHIPS, 8, 128), BF16),
            vmem((512, 512), BF16),
            vmem((512, 512), BF16),
            vmem((2, 512, 128), BF16),
            vmem((2, 512, 128), F32),
            vmem((CHIPS, 8, 128), BF16),
            vmem((1024, 128), F32),
            dma, dma, dma((2,)), dma, dma, dma, dma, dma, pltpu.SemaphoreType.REGULAR,
        ],
        compiler_params=pltpu.CompilerParams(collective_id=0, **params),
        cost_estimate=pl.CostEstimate(
            flops=500_000_000, bytes_accessed=2_000_000, transcendentals=1_000_000
        ),
        name="triangle",
    )(
        pair_act.reshape(1024, 128),
        norm_gain.reshape(1, -1),
        norm_bias.reshape(1, -1),
        proj_weight,
        proj_bias.reshape(1, -1),
        gate_weight,
        gate_bias.reshape(1, -1),
    )
    out = pl.pallas_call(
        finish,
        out_shape=jax.ShapeDtypeStruct((4, 8, 32, 128), BF16),
        in_specs=[pl.BlockSpec(memory_space=pl.ANY)] * 6,
        out_specs=pl.BlockSpec(memory_space=pl.ANY),
        scratch_shapes=[
            vmem((CHIPS, 8, 128), BF16),
            vmem((1024, 128), F32),
            vmem((1, 128), F32),
            vmem((1, 128), F32),
            vmem((128, 128), BF16),
            vmem((1, 128), F32),
            vmem((1024, 128), F32),
            vmem((128, 128), F32),
            vmem((128, 128), F32),
            vmem((4, 8, 32, 128), BF16),
            dma((9,)),
            dma((4,)),
        ],
        compiler_params=pltpu.CompilerParams(vmem_limit_bytes=56 << 20),
        name="finish",
    )(blocks, gate, mid_gain.reshape(1, -1), mid_bias.reshape(1, -1), out_weight, out_bias.reshape(1, -1))
    return out.reshape(32, 32, 128)


def solution(mesh):
    placed = (P("row", "col", None),) + (P(),) * 10
    return jax.shard_map(
        per_device, mesh=mesh, in_specs=placed, out_specs=P("row", "col", None), check_vma=False
    )
```

```python
import jax
import jax.numpy as jnp
from jax import lax
from jax.experimental import pallas as pl
from jax.experimental.pallas import tpu as pltpu
from jax.sharding import PartitionSpec as P

MESH = pl.DeviceIdType.MESH
BF16 = jnp.bfloat16
F32 = jnp.float32
EPS = 1e-05

NX, NY, NZ = 4, 4, 8
CHIPS = NX * NY * NZ


def place():
    row, col = lax.axis_index("row"), lax.axis_index("col")
    core = lax.rem(row, 2)
    y = lax.rem(lax.div(row, 2), NY)
    x = lax.div(col, NZ) * 2 + lax.div(row, 2 * NY)
    return x, y, lax.rem(col, NZ), core


def device(x, y, z, core):
    return lax.rem(x, 2) * 8 + y * 2 + core, lax.div(x, 2) * NZ + z


def transpose_blocks(v, lane):
    low, even = lane < 64, lax.rem(lax.div(lane, 32), 2) == 0
    u0 = jnp.where(low, v[0], pltpu.roll(v[2], 64, 1))
    u2 = jnp.where(low, pltpu.roll(v[0], 64, 1), v[2])
    u1 = jnp.where(low, v[1], pltpu.roll(v[3], 64, 1))
    u3 = jnp.where(low, pltpu.roll(v[1], 64, 1), v[3])
    return (
        jnp.where(even, u0, pltpu.roll(u1, 32, 1)),
        jnp.where(even, pltpu.roll(u0, 96, 1), u1),
        jnp.where(even, u2, pltpu.roll(u3, 32, 1)),
        jnp.where(even, pltpu.roll(u2, 96, 1), u3),
    )


def column(vec, width):
    return jnp.transpose(jnp.broadcast_to(vec, (width, vec.shape[1])))


WAVES = (
    ((1, 4), (1, 3), (1, 5), (0, 4)),
    ((1, 2), (1, 6), (0, 3), (0, 5)),
    ((1, 1), (1, 7), (0, 2), (0, 6)),
    ((1, 0), (0, 1), (0, 7), (0, 0)),
)
TO_CORE = (0, 1, 1, 0)
ROWS = (1, 0, 9, 8, 3, 2, 11, 10, 5, 4, 13, 12, 7, 6, 15, 14)


def kernel(
    x_hbm, ng_hbm, nb_hbm, pw_hbm, pb_hbm, gw_hbm, gb_hbm,
    back_in, gate_hbm,
    x_ref, ng_ref, nb_ref, pw_ref, pb_ref, gw_ref, gb_ref, load_sem,
    xn, wt, pbt, grp_l, grp_r, send_l, send_r, recv_l, mate_l, recv_r, left, left_t, right,
    back, gate,
    send_sem, left_sem, right_sem, mate_send, mate_recv, back_send, back_recv, out_sem, mate_sem,
):
    loads = [
        pltpu.make_async_copy(src, dst, load_sem.at[i])
        for i, (src, dst) in enumerate(
            (
                (x_hbm, x_ref), (ng_hbm, ng_ref), (nb_hbm, nb_ref), (pw_hbm, pw_ref),
                (pb_hbm, pb_ref), (gw_hbm, gw_ref), (gb_hbm, gb_ref),
            )
        )
    ]
    for load in loads:
        load.start()
    x, y, z, core = place()
    rows, cols = device(x, y, z, core)
    slot = lax.div(rows, 2) * 16 + cols
    chan = z * 16 + x * NY + y
    partner = device(x, y, z, 1 - core)
    x_lo, x_hi = lax.rem(x, 2), lax.div(x, 2)

    def send_waves(act, waves=(0, 1, 2, 3)):
        for w in waves:
            wave = WAVES[w]
            chips = []
            for hi, d in wave:
                txh, tz = lax.rem(x_hi + hi, 2), lax.rem(z + d, NZ)
                chips.append(((hi, d) == (0, 0), tz * 16 + txh * 8, txh * NZ + tz))

            def step(i, carry, w=w, chips=chips):
                base = lax.rem(x_lo + 1 + lax.div(i, 4), 2) * NY + lax.rem(y + 2 + i, NY)
                for mine, to_chan, to_col in chips:
                    act(w, jnp.logical_and(i == 6, mine) if mine else None, base, to_chan, to_col)
                return carry

            lax.fori_loop(0, 8, step, 0)

    barrier = pltpu.get_barrier_semaphore()

    def greet(w, mine, base, to_chan, to_col):
        def signal():
            pl.semaphore_signal(
                barrier, inc=1, device_id=(base * 2 + core, to_col), device_id_type=MESH
            )

        if mine is None:
            signal()
        else:
            pl.when(jnp.logical_not(mine))(signal)

    send_waves(greet)
    pl.semaphore_signal(barrier, inc=1, device_id=partner, device_id_type=MESH)

    for load in loads:
        load.wait()
    for t in range(8):
        chunk = pl.ds(t * 128, 128)
        v = x_ref[chunk, :].astype(F32)
        center = v - jnp.mean(v, axis=1, keepdims=True)
        spread = jnp.mean(center * center, axis=1, keepdims=True)
        xn[chunk, :] = (center * lax.rsqrt(spread + EPS) * ng_ref[...] + nb_ref[...]).astype(BF16)
    for b in range(4):
        weight = jnp.transpose(pw_ref[:, b * 128 : (b + 1) * 128])
        bias = column(pb_ref[:, b * 128 : (b + 1) * 128], 128)
        for h in range(2):
            wt[pl.ds(h * 256 + b * 64, 64), :] = weight[h * 64 : (h + 1) * 64]
            pbt[pl.ds(h * 256 + b * 64, 64), :] = bias[h * 64 : (h + 1) * 64]

    def project(h):
        for pair in range(4):
            proj = lax.dot_general(
                wt[pl.ds(h * 256, 256), :],
                xn[pl.ds(pair * 256, 256), :],
                (((1,), (1,)), ((), ())),
                preferred_element_type=F32,
            )
            for s in range(2):
                t = pair * 2 + s
                p = [
                    proj[b * 64 : (b + 1) * 64, s * 128 : (s + 1) * 128]
                    + pbt[pl.ds(h * 256 + b * 64, 64), :]
                    for b in range(4)
                ]
                grp_l[pl.ds(t, 64, stride=8), :] = jax.nn.sigmoid(p[0]) * p[1]
                grp_r[pl.ds(t, 64, stride=8), :] = jax.nn.sigmoid(p[2]) * p[3]
        send_l[pl.ds(h * 64, 64)] = grp_l[...].reshape(64, 8, 128).astype(BF16)
        send_r[pl.ds(h * 64, 64)] = grp_r[...].reshape(64, 8, 128).astype(BF16)

    project(0)
    project(1)

    pl.semaphore_wait(barrier, CHIPS)
    pl.semaphore_signal(mate_sem, inc=1, device_id=partner, device_id_type=MESH)

    def push_left(w, mine, base, to_chan, to_col):
        def go():
            pltpu.make_async_remote_copy(
                src_ref=send_l.at[to_chan + base],
                dst_ref=recv_l.at[slot],
                send_sem=send_sem,
                recv_sem=left_sem,
                device_id=(base * 2 + core, to_col),
                device_id_type=MESH,
            ).start()

        if mine is None:
            go()
        else:
            pl.when(jnp.logical_not(mine))(go)

    def push_right(w, mine, base, to_chan, to_col):
        def go():
            pltpu.make_async_remote_copy(
                src_ref=send_r.at[to_chan + base],
                dst_ref=recv_r.at[core, slot],
                send_sem=send_sem,
                recv_sem=right_sem.at[w // 2],
                device_id=(base * 2 + TO_CORE[w], to_col),
                device_id_type=MESH,
            ).start()

        if mine is None:
            go()
        else:
            pl.when(jnp.logical_not(jnp.logical_and(mine, core == TO_CORE[w])))(go)

    send_waves(push_left, (0, 1, 3, 2))
    pl.semaphore_wait(mate_sem, 1)
    send_waves(push_right, (2, 3, 0, 1))
    recv_l[slot] = send_l[chan]

    @pl.when(core == TO_CORE[3])
    def _():
        pltpu.make_async_copy(send_r.at[chan], recv_r.at[core, slot], right_sem.at[1]).start()

    for t in range(8):
        chunk = pl.ds(t * 128, 128)
        gate[chunk, :] = jax.nn.sigmoid(
            jnp.dot(xn[chunk, :], gw_ref[...], preferred_element_type=F32) + gb_ref[...]
        )
    keep = pltpu.make_async_copy(gate, gate_hbm, out_sem)
    keep.start()

    landed = recv_l.at[pl.ds(0, CHIPS - 1)]
    pltpu.make_async_copy(landed, landed, left_sem).wait()

    swap = pltpu.make_async_remote_copy(
        src_ref=recv_l,
        dst_ref=mate_l,
        send_sem=mate_send,
        recv_sem=mate_recv,
        device_id=partner,
        device_id_type=MESH,
    )
    swap.start()

    lane = lax.broadcasted_iota(jnp.int32, (16, 128), 1)

    def regroup(source, cs, store, row, first):
        for p in range(4):
            tiles = [
                jnp.concatenate(
                    [source[(2 * p + q) * 16 + c].astype(F32) for q in range(2)], axis=0
                )
                for c in cs
            ]
            for k4, tile in enumerate(transpose_blocks(tiles, lane)):
                store[pl.ds(row + k4 * 64 + p * 16, 16), pl.ds(first, 128)] = tile.astype(BF16)

    for half, source in enumerate((recv_l, mate_l)):
        if half == 1:
            swap.wait_recv()
        for g in range(4):
            regroup(source, [4 * g + m for m in range(4)], left, half * 256, g * 128)
        for g in range(4):
            for h in range(2):
                block = left[pl.ds(half * 256 + h * 128, 128), pl.ds(g * 128, 128)]
                left_t[pl.ds(g * 128, 128), pl.ds(half * 256 + h * 128, 128)] = jnp.transpose(block)

    lane8 = lax.broadcasted_iota(jnp.int32, (8, 128), 1)

    def multiply(j):
        arrived = recv_r.at[0, pl.ds(0, 64)]
        pltpu.make_async_copy(arrived, arrived, right_sem.at[j]).wait()
        for half, source in enumerate((recv_r.at[core], recv_r.at[1 - core])):
            regroup(source, came_from[j], right.at[j], half * 256, 0)
        return jnp.dot(left_t[...], right[j], preferred_element_type=F32)

    def give(j, product):
        places = []
        for i in range(16):
            row = ROWS[i]
            tiles = []
            for q in range(4):
                tiles.append(product[row * 32 + q * 8 : row * 32 + q * 8 + 8])
            for m, tile in enumerate(transpose_blocks(tiles, lane8)):
                place_in = j * 64 + i * 4 + m
                back[place_in] = tile.astype(BF16)
                places.append((row, came_from[j][m], place_in, j == 1 and m == 3))
        for row, col, place_in, maybe_here in places:

            def go(row=row, col=col, place_in=place_in):
                pltpu.make_async_remote_copy(
                    src_ref=back.at[place_in],
                    dst_ref=back_in.at[chan],
                    send_sem=back_send,
                    recv_sem=back_recv,
                    device_id=(row, col),
                    device_id_type=MESH,
                ).start()

            if maybe_here:
                here = jnp.logical_and(row == rows, col == cols)
                pl.when(jnp.logical_not(here))(go)

                @pl.when(here)
                def _(place_in=place_in):
                    pltpu.make_async_copy(back.at[place_in], back_in.at[chan], back_recv).start()

            else:
                go()

    came_from = []
    for w0, w1 in ((0, 1), (3, 2)):
        cols_of = []
        for (hi0, d0), (hi1, d1) in zip(WAVES[w0], WAVES[w1]):
            hi, d = jnp.where(core == 0, hi0, hi1), jnp.where(core == 0, d0, d1)
            cols_of.append(lax.rem(x_hi + hi, 2) * NZ + lax.rem(z + NZ - d, NZ))
        came_from.append(cols_of)
    give(1, multiply(1))
    give(0, multiply(0))

    pltpu.make_async_copy(back_in, back_in, back_recv).wait()

    keep.wait()
    swap.wait_send()
    for gone, sem in ((send_l, send_sem), (send_r, send_sem), (back, back_send)):
        most = gone.at[pl.ds(0, CHIPS - 1)]
        pltpu.make_async_copy(most, most, sem).wait()

    @pl.when(core != TO_CORE[3])
    def _():
        for gone, sem in ((send_r, send_sem), (back, back_send)):
            last = gone.at[pl.ds(0, 1)]
            pltpu.make_async_copy(last, last, sem).wait()


def finish(
    back_hbm, gate_hbm, mg_hbm, mb_hbm, ow_hbm, ob_hbm, out_hbm,
    back_in, gate, mg_ref, mb_ref, ow_ref, ob_ref, mixed, mgt, mbt, result, load_sem, out_sem,
):
    pieces = [
        pltpu.make_async_copy(
            back_hbm.at[pl.ds(i * 32, 32)], back_in.at[pl.ds(i * 32, 32)], load_sem.at[i]
        )
        for i in range(4)
    ]
    loads = [
        pltpu.make_async_copy(src, dst, load_sem.at[4 + i])
        for i, (src, dst) in enumerate(
            (
                (mg_hbm, mg_ref), (mb_hbm, mb_ref), (ow_hbm, ow_ref), (ob_hbm, ob_ref),
                (gate_hbm, gate),
            )
        )
    ]
    for load in pieces + loads:
        load.start()
    for load in loads[:2]:
        load.wait()
    mgt[...] = column(mg_ref[...], 128)
    mbt[...] = column(mb_ref[...], 128)
    for load in pieces:
        load.wait()
    values = back_in[...].astype(F32)
    center = values - jnp.mean(values, axis=0, keepdims=True)
    spread = jnp.mean(center * center, axis=0, keepdims=True)
    mixed[...] = (center * lax.rsqrt(spread + EPS)).reshape(1024, 128)
    for load in loads[2:]:
        load.wait()
    writes = []
    for t in range(8):
        norm = mixed[pl.ds(t, 128, stride=8), :] * mgt[...] + mbt[...]
        res = lax.dot_general(
            norm.astype(BF16),
            ow_ref[...],
            (((0,), (0,)), ((), ())),
            preferred_element_type=F32,
        ) + ob_ref[...]
        for q in range(4):
            where = pl.ds(q * 256 + t * 32, 32)
            result[q, t] = (gate[where, :] * res[q * 32 : (q + 1) * 32]).astype(BF16)
        if t % 2:
            pair = pl.ds(t - 1, 2)
            write = pltpu.make_async_copy(
                result.at[:, pair], out_hbm.at[:, pair], out_sem.at[t // 2]
            )
            write.start()
            writes.append(write)

    for write in writes:
        write.wait()


def per_device(
    pair_act, norm_gain, norm_bias, proj_weight, proj_bias, gate_weight, gate_bias, mid_gain,
    mid_bias, out_weight, out_bias,
):
    dma = pltpu.SemaphoreType.DMA
    vmem = pltpu.VMEM
    params = dict(has_side_effects=True, vmem_limit_bytes=56 << 20)
    blocks, gate = pl.pallas_call(
        kernel,
        out_shape=[
            jax.ShapeDtypeStruct((CHIPS, 8, 128), BF16),
            jax.ShapeDtypeStruct((1024, 128), F32),
        ],
        in_specs=[pl.BlockSpec(memory_space=pl.ANY)] * 7,
        out_specs=[pl.BlockSpec(memory_space=pl.ANY)] * 2,
        scratch_shapes=[
            vmem((1024, 128), BF16),
            vmem((1, 128), F32),
            vmem((1, 128), F32),
            vmem((128, 512), BF16),
            vmem((1, 512), F32),
            vmem((128, 128), BF16),
            vmem((1, 128), F32),
            dma((7,)),
            vmem((1024, 128), BF16),
            vmem((512, 128), BF16),
            vmem((512, 128), F32),
            vmem((512, 128), F32),
            vmem((512, 128), F32),
            vmem((CHIPS, 8, 128), BF16),
            vmem((CHIPS, 8, 128), BF16),
            vmem((CHIPS, 8, 128), BF16),
            vmem((CHIPS, 8, 128), BF16),
            vmem((2, CHIPS, 8, 128), BF16),
            vmem((512, 512), BF16),
            vmem((512, 512), BF16),
            vmem((2, 512, 128), BF16),
            vmem((CHIPS, 8, 128), BF16),
            vmem((1024, 128), F32),
            dma, dma, dma((2,)), dma, dma, dma, dma, dma, pltpu.SemaphoreType.REGULAR,
        ],
        compiler_params=pltpu.CompilerParams(collective_id=0, **params),
        cost_estimate=pl.CostEstimate(
            flops=500_000_000, bytes_accessed=2_000_000, transcendentals=1_000_000
        ),
        name="triangle",
    )(
        pair_act.reshape(1024, 128),
        norm_gain.reshape(1, -1),
        norm_bias.reshape(1, -1),
        proj_weight,
        proj_bias.reshape(1, -1),
        gate_weight,
        gate_bias.reshape(1, -1),
    )
    out = pl.pallas_call(
        finish,
        out_shape=jax.ShapeDtypeStruct((4, 8, 32, 128), BF16),
        in_specs=[pl.BlockSpec(memory_space=pl.ANY)] * 6,
        out_specs=pl.BlockSpec(memory_space=pl.ANY),
        scratch_shapes=[
            vmem((CHIPS, 8, 128), BF16),
            vmem((1024, 128), F32),
            vmem((1, 128), F32),
            vmem((1, 128), F32),
            vmem((128, 128), BF16),
            vmem((1, 128), F32),
            vmem((1024, 128), F32),
            vmem((128, 128), F32),
            vmem((128, 128), F32),
            vmem((4, 8, 32, 128), BF16),
            dma((9,)),
            dma((4,)),
        ],
        compiler_params=pltpu.CompilerParams(vmem_limit_bytes=56 << 20),
        name="finish",
    )(blocks, gate, mid_gain.reshape(1, -1), mid_bias.reshape(1, -1), out_weight, out_bias.reshape(1, -1))
    return out.reshape(32, 32, 128)


def solution(mesh):
    placed = (P("row", "col", None),) + (P(),) * 10
    return jax.shard_map(
        per_device, mesh=mesh, in_specs=placed, out_specs=P("row", "col", None), check_vma=False
    )
```
